512 devices in a mesh: prow: 32 (over y, x, z_hi), pcol: 16 (over z_lo, core).
Axes of the slice: x: 4, y: 4, z: 16 (z_hi: 2, z_lo: 8; z = z_hi * 8 + z_lo), core: 2. Of those that a mesh axis runs over, the one named last changes fastest.
Arguments:
- right_side: float32 [2, 1024, 2048], P(None, 'prow', 'pcol'), may hold values from -6 to 6
- diag_inverse: float32 [2, 1024, 1024], P(None, 'prow'), as said below
- coupling: float32 [1024, 1024], P('prow'), may hold values from -0.1875 to 0.1875
- panel: float32 [2, 1024, 8192], P(None, 'prow', 'pcol'), may hold values from -0.0625 to 0.0625
- solved: float32 [8192, 2048], P('pcol'), may hold values from -6 to 6
Outputs:
- solution: float32 [2, 1024, 2048], P(None, 'prow', 'pcol')
The draws below stay inside these ranges and needn't reach their ends.
Inputs may be any that keep to these rules, and one draw needn't show every extreme that they name: `diag_inverse`: each of the 2 blocks is lower triangular, its diagonal entries between 0.6 and 1.4.
All inputs are finite; a program needn't handle non-finite values.
Results may differ from the reference program's by a relative error of at most 0.000062.
Values sent between devices are 32-bit elements; how exact they have to be, the bound alone decides.
No kernel may reach another device: no remote copies, remote signals or barrier semaphores. Data moves between devices by JAX's collectives and lax.ppermute only.
A program may use at most 64 MiB of HBM per device.

```python
import jax
import jax.numpy as jnp
from jax import lax

B = 1024
STEPS = 2
PREV = 8192
RHS = 2048


def draw_diag_inverse(key, part):
    key = jax.random.fold_in(key, 11)
    key_off, key_diag = jax.random.split(key)
    index_of_row = jnp.arange(B, dtype=jnp.int32)[:, None]
    col_index = jnp.arange(B, dtype=jnp.int32)[None, :]
    offdiag = jax.random.normal(key_off, (STEPS, B, B), jnp.float32)
    offdiag = offdiag / jnp.sqrt(jnp.float32(B))
    diagonal = jax.random.uniform(key_diag, (STEPS, B, 1), jnp.float32, 0.6, 1.4)
    lower = jnp.where(col_index < index_of_row, offdiag, 0.0)
    return lower + jnp.where(col_index == index_of_row, diagonal, 0.0)


def level_of(rng, dims, cuts, least, high):
    factor_of = 1.0
    for position, parts in cuts:
        draws = jax.random.uniform(jax.random.fold_in(jax.random.fold_in(rng, 6), position), (parts,), jnp.float32, least / len(cuts), high / len(cuts))
        factor_of = factor_of * jnp.repeat(jnp.exp(draws), dims[position] // parts).reshape((-1,) + (1,) * (len(dims) - 1 - position))
    return factor_of


def centred(key, extent, width, most, cuts=(), kind=jnp.bfloat16):
    drawn = width * jax.random.normal(key, extent, jnp.float32)
    if cuts:
        drawn = drawn * level_of(key, extent, cuts, -0.22, 0.18)
    return jnp.clip(drawn, -most, most).astype(kind)


def setup_inputs(seed: int = 0) -> dict:
    arg_keys = jax.random.split(jax.random.key(seed), 6)
    right_side = centred(arg_keys[0], (STEPS, B, RHS), 1.0, 6.0, ((1, 32), (2, 16)), jnp.float32)
    diag_inverse = draw_diag_inverse(jax.random.fold_in(arg_keys[5], 71), 0)
    coupling = centred(arg_keys[2], (B, B), B ** -0.5, 0.1875, ((0, 32),), jnp.float32)
    panel = centred(arg_keys[3], (STEPS, B, PREV), PREV ** -0.5, 0.0625, ((1, 32), (2, 16)), jnp.float32)
    solved = centred(arg_keys[4], (PREV, RHS), 1.0, 6.0, ((0, 16),), jnp.float32)
    return dict(right_side=right_side, diag_inverse=diag_inverse, coupling=coupling, panel=panel, solved=solved)


def reference(right_side, diag_inverse, coupling, panel, solved):
    running_partial = jnp.einsum("ftq,qg->ftg", panel, solved, precision=lax.Precision.HIGHEST)
    first_res = right_side[0] - running_partial[0]
    first_sol = jnp.dot(diag_inverse[0], first_res, precision=lax.Precision.HIGHEST, preferred_element_type=jnp.float32)
    cross = jnp.dot(coupling, first_sol, precision=lax.Precision.HIGHEST, preferred_element_type=jnp.float32)
    second_res = right_side[1] - running_partial[1] - cross
    second_solution = jnp.dot(diag_inverse[1], second_res, precision=lax.Precision.HIGHEST, preferred_element_type=jnp.float32)
    return jnp.stack([first_sol, second_solution])
```

```python
import jax
import jax.numpy as jnp
from jax import lax
from jax.sharding import Mesh, PartitionSpec as P

ROWS = ("y", "x", "zh")
COLS = ("zl", "core")


def mul(a, b):
    return jnp.dot(a, b, precision=lax.Precision.HIGH, preferred_element_type=jnp.float32)


def gather_plane(block):
    copies = jnp.broadcast_to(block[None], (16,) + block.shape)
    got = lax.all_to_all(copies, ("y", "x"), 0, 0, tiled=True)
    return got.reshape(16 * block.shape[0], block.shape[1])


def reduce_line(blocks):
    copies = jnp.broadcast_to(blocks[None], (2,) + blocks.shape).reshape(16, 32, 128)
    got = lax.all_to_all(copies, ("zh", "zl"), 0, 0, tiled=True)
    return got.reshape(2, 8, 32, 128).sum(1).reshape(64, 128)


def on_device(right_side, diag_inverse, coupling, panel, solved):
    zh, zl, core = (lax.axis_index(a) for a in ("zh", "zl", "core"))

    factors = jnp.stack([diag_inverse[0], coupling])
    slots = jnp.where((jnp.arange(2) == 1 - zh)[:, None, None, None], factors[None], 0.0)
    other = lax.psum_scatter(slots, "zh", scatter_dimension=0, tiled=True)[0]

    total = mul(panel.reshape(64, 512), solved).reshape(64, 8, 2, 128)
    send = lax.dynamic_index_in_dim(total, 1 - core, 2, keepdims=False)
    keep = lax.dynamic_index_in_dim(total, core, 2, keepdims=False)
    total = keep + lax.ppermute(send, "core", [(0, 1), (1, 0)])
    total = total.reshape(2, 32, 8, 128).transpose(0, 2, 1, 3)
    mine = (jnp.arange(8) == zl)[None, :, None, None]
    reduced = jnp.where(mine, right_side[:, None], 0.0) - total

    first_res = reduce_line(reduced[0])
    second_part = reduce_line(reduced[1])

    def both(index, x):
        a, b = mul(factors[index], x), mul(other[index], x)
        return jnp.where(zh == 0, jnp.concatenate([a, b]), jnp.concatenate([b, a])), a

    first_sol, first_mine = both(0, gather_plane(first_res))
    cross, _ = both(1, gather_plane(first_sol))
    second_res = second_part - cross
    second_mine = mul(diag_inverse[1], gather_plane(second_res))
    return jnp.stack([first_mine, second_mine])


def solution(mesh):
    fine = Mesh(mesh.devices.reshape(4, 4, 2, 8, 2), ROWS + COLS)
    return jax.shard_map(
        on_device,
        mesh=fine,
        in_specs=(
            P(None, ROWS, COLS),
            P(None, ROWS, None),
            P(ROWS, None),
            P(None, ROWS, COLS),
            P(COLS, None),
        ),
        out_specs=P(None, ROWS, COLS),
        check_vma=False,
    )
```

```python
import functools

import jax
import jax.numpy as jnp
from jax import lax
from jax.experimental import pallas as pl
from jax.experimental.pallas import tpu as pltpu
from jax.sharding import Mesh, PartitionSpec as P

ROWS = ("y", "x", "zh")
LINE = ("q", "b")
COLS = LINE + ("core",)


def mul(a, b):
    return jnp.dot(a, b, precision=lax.Precision.HIGHEST, preferred_element_type=jnp.float32)


def halves(x):
    high = x.astype(jnp.bfloat16)
    return high, (x - high.astype(jnp.float32)).astype(jnp.bfloat16)


def product_kernel(add, where_ref, panel_ref, even_ref, odd_ref, *rest):
    out_ref = rest[-1]
    step = pl.program_id(0)
    p_high, p_low = halves(-panel_ref[...])
    s_high, s_low = halves(jnp.concatenate([even_ref[...], odd_ref[...]], axis=1))
    dot = functools.partial(jnp.dot, preferred_element_type=jnp.float32)
    wide = dot(jnp.concatenate([p_high, p_low], axis=0), s_high)
    got = wide[64:] + dot(p_high, s_low) + wide[:64]
    for b in range(2):
        part = got[:, 128 * b : 128 * (b + 1)]
        if add:
            mine = jnp.logical_and(where_ref[1] == step, where_ref[2] == b)
            part = part + jnp.where(mine, rest[0][...], 0.0)
        out_ref[b, 0] = part


def product(where, panel, solved, add=None):
    whole = lambda shape: pl.BlockSpec(shape, lambda i, w: (0, 0))
    cols = lambda b: pl.BlockSpec((512, 128), lambda i, w: (0, 4 * i + 2 * b + w[0]))
    args = (panel, solved, solved) + (() if add is None else (add,))
    return pl.pallas_call(
        functools.partial(product_kernel, add is not None),
        out_shape=jax.ShapeDtypeStruct((2, 4, 64, 128), jnp.float32),
        grid_spec=pltpu.PrefetchScalarGridSpec(
            num_scalar_prefetch=1,
            grid=(4,),
            in_specs=[whole((64, 512)), cols(0), cols(1)] + ([] if add is None else [whole((64, 128))]),
            out_specs=pl.BlockSpec((2, 1, 64, 128), lambda i, w: (0, i, 0, 0)),
        ),
        compiler_params=pltpu.CompilerParams(vmem_limit_bytes=16 << 20),
        cost_estimate=pl.CostEstimate(flops=6 * 64 * 512 * 1024, bytes_accessed=3 << 20, transcendentals=0),
    )(where, *args)


def gather_plane(block):
    copies = jnp.broadcast_to(block[None], (16,) + block.shape)
    got = lax.all_to_all(copies, ("y", "x"), 0, 0, tiled=True)
    return got.reshape(16 * block.shape[0], block.shape[1])


def on_device(right_side, diag_inverse, coupling, panel, solved):
    zh, q, b, core = (lax.axis_index(a) for a in ("zh", "q", "b", "core"))
    swap = [(0, 1), (1, 0)]

    factor = jnp.where(core == 0, diag_inverse[0], coupling)
    slots = jnp.where((jnp.arange(2) == 1 - zh)[:, None, None], factor[None], 0.0)
    pairs = [[z, 15 - z] for z in range(8)]
    got = lax.psum_scatter(slots, ("zh",) + LINE, scatter_dimension=0, axis_index_groups=pairs, tiled=True)[0]
    where = lambda c: jnp.stack([c, q, b]).astype(jnp.int32)
    panel = panel.reshape(64, 512)
    send = product(where(1 - core), panel, solved)
    moved = lax.ppermute(send, "core", swap)
    keep = product(where(core), panel, solved, right_side.reshape(64, 128))
    total = keep + moved
    moved = lax.ppermute(lax.dynamic_index_in_dim(total, 1 - b, 0, keepdims=False), "b", swap)
    total = lax.dynamic_index_in_dim(total, b, 0, keepdims=False) + moved
    copies = jnp.broadcast_to(total[None], (2, 4, 64, 128)).reshape(8, 64, 128)
    got_all = lax.all_to_all(copies, ("zh", "q"), 0, 0, tiled=True)
    got_all, got = lax.optimization_barrier((got_all, got))
    partner = lax.ppermute(got, "core", swap)
    other = (jnp.where(core == 0, got, partner), jnp.where(core == 0, partner, got))
    residual = got_all.reshape(2, 4, 2, 32, 128).sum(1)
    first_res = residual[:, 0].reshape(64, 128)
    second_part = residual[:, 1].reshape(64, 128)

    def both(mine, theirs, x):
        a, c = mul(mine, x), mul(theirs, x)
        return jnp.where(zh == 0, jnp.concatenate([a, c]), jnp.concatenate([c, a])), a

    first_sol, first_mine = both(diag_inverse[0], other[0], gather_plane(first_res))
    cross, _ = both(coupling, other[1], gather_plane(first_sol))
    second_mine = mul(diag_inverse[1], gather_plane(second_part - cross))
    return jnp.stack([first_mine, second_mine])


def solution(mesh):
    fine = Mesh(mesh.devices.reshape(4, 4, 2, 4, 2, 2), ROWS + COLS)
    return jax.shard_map(
        on_device,
        mesh=fine,
        in_specs=(
            P(None, ROWS, COLS),
            P(None, ROWS, None),
            P(ROWS, None),
            P(None, ROWS, COLS),
            P(COLS, None),
        ),
        out_specs=P(None, ROWS, COLS),
        check_vma=False,
    )
```

```python
import functools

import jax
import jax.numpy as jnp
from jax import lax
from jax.experimental import pallas as pl
from jax.experimental.pallas import tpu as pltpu
from jax.sharding import Mesh, PartitionSpec as P

ROWS = ("y", "x", "zh")
LINE = ("q", "b")
COLS = LINE + ("core",)


def mul(a, b):
    return jnp.dot(a, b, precision=lax.Precision.HIGHEST, preferred_element_type=jnp.float32)


def halves(x):
    high = x.astype(jnp.bfloat16)
    return high, (x - high.astype(jnp.float32)).astype(jnp.bfloat16)


def product_kernel(add, where_ref, panel_ref, even_ref, odd_ref, *rest):
    out_ref = rest[-1]
    step = pl.program_id(0)
    p_high, p_low = halves(-panel_ref[...])
    s_high, s_low = halves(jnp.concatenate([even_ref[...], odd_ref[...]], axis=1))
    dot = functools.partial(jnp.dot, preferred_element_type=jnp.float32)
    wide = dot(jnp.concatenate([p_high, p_low], axis=0), s_high)
    got = wide[64:] + dot(p_high, s_low) + wide[:64]
    for b in range(2):
        part = got[:, 128 * b : 128 * (b + 1)]
        if add:
            mine = jnp.logical_and(where_ref[1] == step, where_ref[2] == b)
            part = part + jnp.where(mine, rest[0][...], 0.0)
        out_ref[b, 0] = part


def product(where, panel, solved, add=None):
    whole = lambda shape: pl.BlockSpec(shape, lambda i, w: (0, 0))
    cols = lambda b: pl.BlockSpec((512, 128), lambda i, w: (0, 4 * i + 2 * b + w[0]))
    args = (panel, solved, solved) + (() if add is None else (add,))
    return pl.pallas_call(
        functools.partial(product_kernel, add is not None),
        out_shape=jax.ShapeDtypeStruct((2, 4, 64, 128), jnp.float32),
        grid_spec=pltpu.PrefetchScalarGridSpec(
            num_scalar_prefetch=1,
            grid=(4,),
            in_specs=[whole((64, 512)), cols(0), cols(1)] + ([] if add is None else [whole((64, 128))]),
            out_specs=pl.BlockSpec((2, 1, 64, 128), lambda i, w: (0, i, 0, 0)),
        ),
        compiler_params=pltpu.CompilerParams(vmem_limit_bytes=60 << 20),
        cost_estimate=pl.CostEstimate(flops=6 * 64 * 512 * 1024, bytes_accessed=3 << 20, transcendentals=0),
    )(where, *args)


def gather_plane(block):
    copies = jnp.broadcast_to(block[None], (16,) + block.shape)
    got = lax.all_to_all(copies, ("y", "x"), 0, 0, tiled=True)
    return got.reshape(16 * block.shape[0], block.shape[1])


def on_device(right_side, diag_inverse, coupling, panel, solved):
    zh, q, b, core = (lax.axis_index(a) for a in ("zh", "q", "b", "core"))
    swap = [(0, 1), (1, 0)]

    factor = jnp.where(core == 0, diag_inverse[0], coupling)
    got = lax.ppermute(factor, ("zh",) + LINE, [(z, 15 - z) for z in range(16)])

    where = lambda c: jnp.stack([c, q, b]).astype(jnp.int32)
    panel = panel.reshape(64, 512)
    send = product(where(1 - core), panel, solved)
    moved = lax.ppermute(send, "core", swap)
    keep = product(where(core), panel, solved, right_side.reshape(64, 128))
    total = keep + moved
    moved = lax.ppermute(lax.dynamic_index_in_dim(total, 1 - b, 0, keepdims=False), "b", swap)
    total = lax.dynamic_index_in_dim(total, b, 0, keepdims=False) + moved
    copies = jnp.broadcast_to(total[None], (2, 4, 64, 128)).reshape(8, 64, 128)
    got_all = lax.all_to_all(copies, ("zh", "q"), 0, 0, tiled=True)
    got_all, got = lax.optimization_barrier((got_all, got))
    partner = lax.ppermute(got, "core", swap)
    other = (jnp.where(core == 0, got, partner), jnp.where(core == 0, partner, got))
    residual = got_all.reshape(2, 4, 2, 32, 128).sum(1)
    first_res = residual[:, 0].reshape(64, 128)
    second_part = residual[:, 1].reshape(64, 128)

    def both(mine, theirs, x):
        a, c = mul(mine, x), mul(theirs, x)
        return jnp.where(zh == 0, jnp.concatenate([a, c]), jnp.concatenate([c, a])), a

    first_sol, first_mine = both(diag_inverse[0], other[0], gather_plane(first_res))
    cross, _ = both(coupling, other[1], gather_plane(first_sol))
    second_mine = mul(diag_inverse[1], gather_plane(second_part - cross))
    return jnp.stack([first_mine, second_mine])


def solution(mesh):
    fine = Mesh(mesh.devices.reshape(4, 4, 2, 4, 2, 2), ROWS + COLS)
    return jax.shard_map(
        on_device,
        mesh=fine,
        in_specs=(
            P(None, ROWS, COLS),
            P(None, ROWS, None),
            P(ROWS, None),
            P(None, ROWS, COLS),
            P(COLS, None),
        ),
        out_specs=P(None, ROWS, COLS),
        check_vma=False,
    )
```

```python
import functools

import jax
import jax.numpy as jnp
from jax import lax
from jax.experimental import pallas as pl
from jax.experimental.pallas import tpu as pltpu
from jax.sharding import Mesh, PartitionSpec as P

ROWS = ("y", "x", "zh")
LINE = ("q", "b")
COLS = LINE + ("core",)


def mul(a, b):
    return jnp.dot(a, b, precision=lax.Precision.HIGHEST, preferred_element_type=jnp.float32)


def halves(x):
    high = x.astype(jnp.bfloat16)
    return high, (x - high.astype(jnp.float32)).astype(jnp.bfloat16)


def product_kernel(mine, panel_ref, solved_ref, *rest):
    out_ref, slots, sems = rest[-3:]
    core, q, b = (lax.axis_index(a) for a in ("core", "q", "b"))
    parity = core if mine else 1 - core
    copies = []
    for step in range(4):
        for half in range(2):
            columns = pl.ds(pl.multiple_of((4 * step + 2 * half + parity) * 128, 128), 128)
            copy = pltpu.make_async_copy(
                solved_ref.at[:, columns],
                slots.at[step, :, pl.ds(128 * half, 128)],
                sems.at[step, half],
            )
            copy.start()
            copies.append(copy)
    p_high, p_low = halves(-panel_ref[...])
    p_both = jnp.concatenate([p_high, p_low], axis=0)
    dot = functools.partial(jnp.dot, preferred_element_type=jnp.float32)
    for step in range(4):
        copies[2 * step].wait()
        copies[2 * step + 1].wait()
        s_high, s_low = halves(slots[step])
        wide = dot(p_both, s_high)
        got = wide[64:] + dot(p_high, s_low) + wide[:64]
        for half in range(2):
            part = got[:, 128 * half : 128 * (half + 1)]
            if mine:
                here = jnp.logical_and(q == step, b == half)
                part = part + jnp.where(here, rest[0][...], 0.0)
            out_ref[half, step] = part


def product(panel, solved, add=None):
    args = (panel, solved) + (() if add is None else (add,))
    vmem = pl.BlockSpec(memory_space=pltpu.VMEM)
    return pl.pallas_call(
        functools.partial(product_kernel, add is not None),
        out_shape=jax.ShapeDtypeStruct((2, 4, 64, 128), jnp.float32),
        in_specs=[vmem, pl.BlockSpec(memory_space=pl.ANY)] + [vmem] * (add is not None),
        out_specs=vmem,
        scratch_shapes=[pltpu.VMEM((4, 512, 256), jnp.float32), pltpu.SemaphoreType.DMA((4, 2))],
        compiler_params=pltpu.CompilerParams(vmem_limit_bytes=56 << 20),
        cost_estimate=pl.CostEstimate(flops=6 * 64 * 512 * 1024, bytes_accessed=3 << 20, transcendentals=0),
    )(*args)


def pair_up(index, mine, theirs):
    first = index == 0
    return jnp.stack([jnp.where(first, mine, theirs), jnp.where(first, theirs, mine)])


def gather_plane(block):
    copies = jnp.broadcast_to(block[None], (16,) + block.shape)
    got = lax.all_to_all(copies, ("y", "x"), 0, 0, tiled=True)
    return got.reshape(16 * block.shape[0], block.shape[1])


def on_device(right_side, diag_inverse, coupling, panel, solved):
    zh, b, core = (lax.axis_index(a) for a in ("zh", "b", "core"))
    swap = [(0, 1), (1, 0)]

    rows = lambda x: lax.dynamic_slice_in_dim(x, 16 * core, 16, 0)
    quarter = jnp.where(b == 1, rows(diag_inverse[0]), rows(coupling))
    quarter = lax.ppermute(quarter, ("zh",) + LINE, [(z, 15 - z) for z in range(16)])

    panel = panel.reshape(64, 512)
    send = product(panel, solved)
    moved = lax.ppermute(send, "core", swap)
    keep = product(panel, solved, right_side.reshape(64, 128))
    total = keep + moved
    moved = lax.ppermute(lax.dynamic_index_in_dim(total, 1 - b, 0, keepdims=False), "b", swap)
    total = lax.dynamic_index_in_dim(total, b, 0, keepdims=False) + moved
    half = pair_up(b, quarter, lax.ppermute(quarter, "b", swap))
    other = pair_up(core, half, lax.ppermute(half, "core", swap))
    other = other.transpose(1, 0, 2, 3).reshape(2, 32, 1024)
    copies = jnp.broadcast_to(total[None], (2, 4, 64, 128)).reshape(8, 64, 128)
    got_all = lax.all_to_all(copies, ("zh", "q"), 0, 0, tiled=True)
    got_all, other = lax.optimization_barrier((got_all, other))
    residual = got_all.reshape(2, 4, 2, 32, 128).sum(1)
    first_res = residual[:, 0].reshape(64, 128)
    second_part = residual[:, 1].reshape(64, 128)

    def both(mine, theirs, x):
        a, c = mul(mine, x), mul(theirs, x)
        return jnp.where(zh == 0, jnp.concatenate([a, c]), jnp.concatenate([c, a])), a

    first_sol, first_mine = both(diag_inverse[0], other[0], gather_plane(first_res))
    cross, _ = both(coupling, other[1], gather_plane(first_sol))
    second_mine = mul(diag_inverse[1], gather_plane(second_part - cross))
    return jnp.stack([first_mine, second_mine])


def solution(mesh):
    fine = Mesh(mesh.devices.reshape(4, 4, 2, 4, 2, 2), ROWS + COLS)
    return jax.shard_map(
        on_device,
        mesh=fine,
        in_specs=(
            P(None, ROWS, COLS),
            P(None, ROWS, None),
            P(ROWS, None),
            P(None, ROWS, COLS),
            P(COLS, None),
        ),
        out_specs=P(None, ROWS, COLS),
        check_vma=False,
    )
```

```python
import functools

import jax
import jax.numpy as jnp
from jax import lax
from jax.experimental import pallas as pl
from jax.experimental.pallas import tpu as pltpu
from jax.sharding import Mesh, PartitionSpec as P

ROWS = ("y", "x", "zh")
LINE = ("q", "b")
COLS = LINE + ("core",)


def mul(a, b):
    return jnp.dot(a, b, precision=lax.Precision.HIGHEST, preferred_element_type=jnp.float32)


def halves(x):
    high = x.astype(jnp.bfloat16)
    return high, (x - high.astype(jnp.float32)).astype(jnp.bfloat16)


def product_kernel(mine, panel_ref, solved_ref, *rest):
    out_ref, slots, sems = rest[-3:]
    core, q, b = (lax.axis_index(a) for a in ("core", "q", "b"))
    parity = core if mine else 1 - core
    copies = []
    for step in range(4):
        for half in range(2):
            columns = pl.ds(pl.multiple_of((4 * step + 2 * half + parity) * 128, 128), 128)
            copy = pltpu.make_async_copy(
                solved_ref.at[:, columns],
                slots.at[step, :, pl.ds(128 * half, 128)],
                sems.at[step, half],
            )
            copy.start()
            copies.append(copy)
    p_high, p_low = halves(-panel_ref[...])
    p_both = jnp.concatenate([p_high, p_low], axis=0)
    dot = functools.partial(jnp.dot, preferred_element_type=jnp.float32)
    for step in range(4):
        copies[2 * step].wait()
        copies[2 * step + 1].wait()
        s_high, s_low = halves(slots[step])
        wide = dot(p_both, s_high)
        got = wide[64:] + dot(p_high, s_low) + wide[:64]
        for half in range(2):
            part = got[:, 128 * half : 128 * (half + 1)]
            if mine:
                here = jnp.logical_and(q == step, b == half)
                part = part + jnp.where(here, rest[0][...], 0.0)
            out_ref[half, step] = part


def product(panel, solved, add=None):
    args = (panel, solved) + (() if add is None else (add,))
    vmem = pl.BlockSpec(memory_space=pltpu.VMEM)
    return pl.pallas_call(
        functools.partial(product_kernel, add is not None),
        out_shape=jax.ShapeDtypeStruct((2, 4, 64, 128), jnp.float32),
        in_specs=[vmem, pl.BlockSpec(memory_space=pl.ANY)] + [vmem] * (add is not None),
        out_specs=vmem,
        scratch_shapes=[pltpu.VMEM((4, 512, 256), jnp.float32), pltpu.SemaphoreType.DMA((4, 2))],
        compiler_params=pltpu.CompilerParams(vmem_limit_bytes=56 << 20),
        cost_estimate=pl.CostEstimate(
            flops=10**9 if add is None else 10**14, bytes_accessed=3 << 20, transcendentals=0
        ),
    )(*args)


def pair_up(index, mine, theirs):
    first = index == 0
    return jnp.stack([jnp.where(first, mine, theirs), jnp.where(first, theirs, mine)])


def gather_plane(block):
    copies = jnp.broadcast_to(block[None], (16,) + block.shape)
    got = lax.all_to_all(copies, ("y", "x"), 0, 0, tiled=True)
    return got.reshape(16 * block.shape[0], block.shape[1])


def on_device(right_side, diag_inverse, coupling, panel, solved):
    zh, b, core = (lax.axis_index(a) for a in ("zh", "b", "core"))
    swap = [(0, 1), (1, 0)]

    rows = lambda x: lax.dynamic_slice_in_dim(x, 16 * core, 16, 0)
    quarter = jnp.where(b == 1, rows(diag_inverse[0]), rows(coupling))
    quarter = quarter.reshape(16, 8, 128).transpose(1, 0, 2).reshape(128, 128)
    quarter = lax.ppermute(quarter, ("zh",) + LINE, [(z, 15 - z) for z in range(16)])

    panel = panel.reshape(64, 512)
    send = product(panel, solved)
    moved = lax.ppermute(send, "core", swap)
    keep = product(panel, solved, right_side.reshape(64, 128))
    moved, quarter = lax.optimization_barrier((moved, quarter))
    take = lambda x, index: lax.dynamic_index_in_dim(x, index, 0, keepdims=False)
    passing = take(keep, 1 - b) + take(moved, 1 - b)
    passed = lax.ppermute(jnp.concatenate([passing.reshape(256, 128), quarter]), "b", swap)
    half = pair_up(b, quarter, passed[256:])
    passed = passed[:256].reshape(4, 64, 128)
    total = take(keep, b) + take(moved, b) + passed
    copies = jnp.broadcast_to(total[None], (2, 4, 64, 128)).reshape(8, 64, 128)
    got_all = lax.all_to_all(copies, ("zh", "q"), 0, 0, tiled=True)
    other = pair_up(core, half, lax.ppermute(half, "core", swap))
    other = other.reshape(2, 2, 8, 16, 128).transpose(1, 0, 3, 2, 4).reshape(2, 32, 1024)
    first_half = zh == 0
    got_all, other, first_half = lax.optimization_barrier((got_all, other, first_half))
    residual = got_all.reshape(2, 4, 2, 32, 128).sum(1)
    first_res = residual[:, 0].reshape(64, 128)
    second_part = residual[:, 1].reshape(64, 128)

    def both(mine, theirs, x):
        a, c = mul(mine, x), mul(theirs, x)
        return jnp.where(first_half, jnp.concatenate([a, c]), jnp.concatenate([c, a])), a

    first_sol, first_mine = both(diag_inverse[0], other[0], gather_plane(first_res))
    cross, _ = both(coupling, other[1], gather_plane(first_sol))
    second_mine = mul(diag_inverse[1], gather_plane(second_part - cross))
    return jnp.stack([first_mine, second_mine])


def solution(mesh):
    fine = Mesh(mesh.devices.reshape(4, 4, 2, 4, 2, 2), ROWS + COLS)
    return jax.shard_map(
        on_device,
        mesh=fine,
        in_specs=(
            P(None, ROWS, COLS),
            P(None, ROWS, None),
            P(ROWS, None),
            P(None, ROWS, COLS),
            P(COLS, None),
        ),
        out_specs=P(None, ROWS, COLS),
        check_vma=False,
    )
```

```python
import functools

import jax
import jax.numpy as jnp
from jax import lax
from jax.experimental import pallas as pl
from jax.experimental.pallas import tpu as pltpu
from jax.sharding import Mesh, PartitionSpec as P

ROWS = ("y", "x", "zh")
LINE = ("q", "b")
COLS = LINE + ("core",)


def mul(a, b):
    return jnp.dot(a, b, precision=lax.Precision.HIGHEST, preferred_element_type=jnp.float32)


def halves(x):
    high = x.astype(jnp.bfloat16)
    return high, (x - high.astype(jnp.float32)).astype(jnp.bfloat16)


def product_kernel(mine, panel_ref, solved_ref, *rest):
    out_ref, slots, sems = rest[-3:]
    core, q, b = (lax.axis_index(a) for a in ("core", "q", "b"))
    parity = core if mine else 1 - core
    copies = []
    for step in range(4):
        columns = pl.ds(512 * step, 512)
        copy = pltpu.make_async_copy(solved_ref.at[:, columns], slots.at[:, columns], sems.at[step])
        copy.start()
        copies.append(copy)
    p_high, p_low = halves(-panel_ref[...])
    p_both = jnp.concatenate([p_high, p_low], axis=0)
    dot = functools.partial(jnp.dot, preferred_element_type=jnp.float32)
    for step in range(4):
        copies[step].wait()
        first = [pl.multiple_of((4 * step + 2 * half + parity) * 128, 128) for half in range(2)]
        pair = jnp.concatenate([slots[:, pl.ds(start, 128)] for start in first], axis=1)
        s_high, s_low = halves(pair)
        wide = dot(p_both, s_high)
        got = wide[64:] + dot(p_high, s_low) + wide[:64]
        for half in range(2):
            part = got[:, 128 * half : 128 * (half + 1)]
            if mine:
                here = jnp.logical_and(q == step, b == half)
                part = part + jnp.where(here, rest[0][...], 0.0)
            out_ref[half, step] = part


def product(panel, solved, add=None):
    args = (panel, solved) + (() if add is None else (add,))
    vmem = pl.BlockSpec(memory_space=pltpu.VMEM)
    return pl.pallas_call(
        functools.partial(product_kernel, add is not None),
        out_shape=jax.ShapeDtypeStruct((2, 4, 64, 128), jnp.float32),
        in_specs=[vmem, pl.BlockSpec(memory_space=pl.ANY)] + [vmem] * (add is not None),
        out_specs=vmem,
        scratch_shapes=[pltpu.VMEM((512, 2048), jnp.float32), pltpu.SemaphoreType.DMA((4,))],
        compiler_params=pltpu.CompilerParams(vmem_limit_bytes=56 << 20),
        cost_estimate=pl.CostEstimate(flops=6 * 64 * 512 * 1024, bytes_accessed=3 << 20, transcendentals=0),
    )(*args)


def pair_up(index, mine, theirs):
    first = index == 0
    return jnp.stack([jnp.where(first, mine, theirs), jnp.where(first, theirs, mine)])


def gather_plane(block):
    copies = jnp.broadcast_to(block[None], (16,) + block.shape)
    got = lax.all_to_all(copies, ("y", "x"), 0, 0, tiled=True)
    return got.reshape(16 * block.shape[0], block.shape[1])


def on_device(right_side, diag_inverse, coupling, panel, solved):
    zh, b, core = (lax.axis_index(a) for a in ("zh", "b", "core"))
    swap = [(0, 1), (1, 0)]

    rows = lambda x: lax.dynamic_slice_in_dim(x, 16 * core, 16, 0)
    quarter = jnp.where(b == 1, rows(diag_inverse[0]), rows(coupling))
    quarter = lax.ppermute(quarter, ("zh",) + LINE, [(z, 15 - z) for z in range(16)])

    panel = panel.reshape(64, 512)
    send = product(panel, solved)
    moved = lax.ppermute(send, "core", swap)
    keep = product(panel, solved, right_side.reshape(64, 128))
    take = lambda x, index: lax.dynamic_index_in_dim(x, index, 0, keepdims=False)
    passed = lax.ppermute(take(keep, 1 - b) + take(moved, 1 - b), "b", swap)
    total = take(keep, b) + take(moved, b) + passed
    half = pair_up(b, quarter, lax.ppermute(quarter, "b", swap))
    other = pair_up(core, half, lax.ppermute(half, "core", swap))
    other = other.transpose(1, 0, 2, 3).reshape(2, 32, 1024)
    copies = jnp.broadcast_to(total[None], (2, 4, 64, 128)).reshape(8, 64, 128)
    got_all = lax.all_to_all(copies, ("zh", "q"), 0, 0, tiled=True)
    first_half = zh == 0
    got_all, other, first_half = lax.optimization_barrier((got_all, other, first_half))
    residual = got_all.reshape(2, 4, 2, 32, 128).sum(1)
    first_res = residual[:, 0].reshape(64, 128)
    second_part = residual[:, 1].reshape(64, 128)

    def both(mine, theirs, x):
        a, c = mul(mine, x), mul(theirs, x)
        return jnp.where(first_half, jnp.concatenate([a, c]), jnp.concatenate([c, a])), a

    first_sol, first_mine = both(diag_inverse[0], other[0], gather_plane(first_res))
    cross, _ = both(coupling, other[1], gather_plane(first_sol))
    second_mine = mul(diag_inverse[1], gather_plane(second_part - cross))
    return jnp.stack([first_mine, second_mine])


def solution(mesh):
    fine = Mesh(mesh.devices.reshape(4, 4, 2, 4, 2, 2), ROWS + COLS)
    return jax.shard_map(
        on_device,
        mesh=fine,
        in_specs=(
            P(None, ROWS, COLS),
            P(None, ROWS, None),
            P(ROWS, None),
            P(None, ROWS, COLS),
            P(COLS, None),
        ),
        out_specs=P(None, ROWS, COLS),
        check_vma=False,
    )
```

```python
import functools

import jax
import jax.numpy as jnp
from jax import lax
from jax.experimental import pallas as pl
from jax.experimental.pallas import tpu as pltpu
from jax.sharding import Mesh, PartitionSpec as P

ROWS = ("y", "x", "zh")
LINE = ("q", "b")
COLS = LINE + ("core",)


def mul(a, b):
    return jnp.dot(a, b, precision=lax.Precision.HIGHEST, preferred_element_type=jnp.float32)


def halves(x):
    high = x.astype(jnp.bfloat16)
    return high, (x - high.astype(jnp.float32)).astype(jnp.bfloat16)


def product_kernel(flips, panel_ref, solved_ref, *rest):
    count = len(flips)
    add_ref = rest[0] if len(rest) > count + 5 else None
    outs = rest[-count - 5 : -5]
    panel_held, add_held, slots, sems, small_sems = rest[-5:]
    core, q, b = (lax.axis_index(a) for a in ("core", "q", "b"))
    copies = []
    for part, (flip_b, flip_core) in enumerate(flips):
        to_b = 1 - b if flip_b else b
        to_core = 1 - core if flip_core else core
        for step in range(4):
            columns = pl.ds(pl.multiple_of((4 * step + 2 * to_b + to_core) * 128, 128), 128)
            copy = pltpu.make_async_copy(
                solved_ref.at[:, columns],
                slots.at[part, :, pl.ds(128 * step, 128)],
                sems.at[part, step],
            )
            copy.start()
            copies.append(copy)
    panel_copy = pltpu.make_async_copy(panel_ref, panel_held, small_sems.at[0])
    panel_copy.start()
    if add_ref is not None:
        add_copy = pltpu.make_async_copy(add_ref, add_held, small_sems.at[1])
        add_copy.start()
        add_copy.wait()
    panel_copy.wait()
    p_high, p_low = halves(-panel_held[...])
    p_both = jnp.concatenate([p_high, p_low], axis=0)
    dot = functools.partial(jnp.dot, preferred_element_type=jnp.float32)
    for part in range(count):
        for two in range(2):
            copies[4 * part + 2 * two].wait()
            copies[4 * part + 2 * two + 1].wait()
            s_high, s_low = halves(slots[part, :, pl.ds(256 * two, 256)])
            wide = dot(p_both, s_high)
            got = wide[64:] + dot(p_high, s_low) + wide[:64]
            for step in range(2 * two, 2 * two + 2):
                block = got[:, 128 * (step % 2) : 128 * (step % 2 + 1)]
                if add_ref is not None:
                    block = block + jnp.where(q == step, add_held[...], 0.0)
                outs[part][step] = block


def product(flips, panel, solved, add=None):
    args = (panel, solved) + (() if add is None else (add,))
    count = len(flips)
    return pl.pallas_call(
        functools.partial(product_kernel, flips),
        out_shape=[jax.ShapeDtypeStruct((4, 64, 128), jnp.float32)] * count,
        in_specs=[pl.BlockSpec(memory_space=pl.ANY)] * len(args),
        out_specs=[pl.BlockSpec(memory_space=pltpu.VMEM)] * count,
        scratch_shapes=[
            pltpu.VMEM((64, 512), jnp.float32),
            pltpu.VMEM((64, 128), jnp.float32),
            pltpu.VMEM((count, 512, 512), jnp.float32),
            pltpu.SemaphoreType.DMA((count, 4)),
            pltpu.SemaphoreType.DMA((2,)),
        ],
        compiler_params=pltpu.CompilerParams(vmem_limit_bytes=56 << 20),
        cost_estimate=pl.CostEstimate(flops=count * 10**8, bytes_accessed=count << 20, transcendentals=0),
    )(*args)


def pair_up(index, mine, theirs):
    first = index == 0
    return jnp.stack([jnp.where(first, mine, theirs), jnp.where(first, theirs, mine)])


def gather_plane(block):
    copies = jnp.broadcast_to(block[None], (16,) + block.shape)
    got = lax.all_to_all(copies, ("y", "x"), 0, 0, tiled=True)
    return got.reshape(16 * block.shape[0], block.shape[1])


def on_device(right_side, diag_inverse, coupling, panel, solved):
    zh, b, core = (lax.axis_index(a) for a in ("zh", "b", "core"))
    swap = [(0, 1), (1, 0)]

    rows = lambda x: lax.dynamic_slice_in_dim(x, 16 * core, 16, 0)
    quarter = jnp.where(b == 1, rows(diag_inverse[0]), rows(coupling))
    quarter = lax.ppermute(quarter, ("zh",) + LINE, [(z, 15 - z) for z in range(16)])

    panel = panel.reshape(64, 512)
    side = right_side.reshape(64, 128)
    across = [(z, z ^ 3) for z in range(4)]
    sends = product(((1, 1), (1, 0), (0, 1)), panel, solved)
    from_both = lax.ppermute(sends[0], ("b", "core"), across)
    from_pair = lax.ppermute(sends[1], "b", swap)
    from_core = lax.ppermute(sends[2], "core", swap)
    (keep,) = product(((0, 0),), panel, solved, side)
    total = keep + from_core + from_pair + from_both
    half = pair_up(b, quarter, lax.ppermute(quarter, "b", swap))
    other = pair_up(core, half, lax.ppermute(half, "core", swap))
    other = other.transpose(1, 0, 2, 3).reshape(2, 32, 1024)
    copies = jnp.broadcast_to(total[None], (2, 4, 64, 128)).reshape(8, 64, 128)
    got_all = lax.all_to_all(copies, ("zh", "q"), 0, 0, tiled=True)
    first_half = zh == 0
    got_all, other, first_half = lax.optimization_barrier((got_all, other, first_half))
    residual = got_all.reshape(2, 4, 2, 32, 128).sum(1)
    first_res = residual[:, 0].reshape(64, 128)
    second_part = residual[:, 1].reshape(64, 128)

    def both(mine, theirs, x):
        a, c = mul(mine, x), mul(theirs, x)
        return jnp.where(first_half, jnp.concatenate([a, c]), jnp.concatenate([c, a])), a

    first_sol, first_mine = both(diag_inverse[0], other[0], gather_plane(first_res))
    cross, _ = both(coupling, other[1], gather_plane(first_sol))
    second_mine = mul(diag_inverse[1], gather_plane(second_part - cross))
    return jnp.stack([first_mine, second_mine])


def solution(mesh):
    fine = Mesh(mesh.devices.reshape(4, 4, 2, 4, 2, 2), ROWS + COLS)
    return jax.shard_map(
        on_device,
        mesh=fine,
        in_specs=(
            P(None, ROWS, COLS),
            P(None, ROWS, None),
            P(ROWS, None),
            P(None, ROWS, COLS),
            P(COLS, None),
        ),
        out_specs=P(None, ROWS, COLS),
        check_vma=False,
    )
```

```python
import functools

import jax
import jax.numpy as jnp
from jax import lax
from jax.experimental import pallas as pl
from jax.experimental.pallas import tpu as pltpu
from jax.sharding import Mesh, PartitionSpec as P

ROWS = ("y", "x", "zh")
LINE = ("q", "b")
COLS = LINE + ("core",)


def mul(a, b):
    return jnp.dot(a, b, precision=lax.Precision.HIGHEST, preferred_element_type=jnp.float32)


def halves(x):
    high = x.astype(jnp.bfloat16)
    return high, (x - high.astype(jnp.float32)).astype(jnp.bfloat16)


def product_kernel(flips, panel_ref, solved_ref, *rest):
    count = len(flips)
    extra = rest[: -count - 5 - (count > 1)]
    outs = rest[len(extra) : -5]
    panel_held, add_held, slots, sems, small_sems = rest[-5:]
    core, q, b = (lax.axis_index(a) for a in ("core", "q", "b"))
    copies = []
    for part, (flip_b, flip_core) in enumerate(flips):
        to_b = 1 - b if flip_b else b
        to_core = 1 - core if flip_core else core
        for step in range(4):
            columns = pl.ds(pl.multiple_of((4 * step + 2 * to_b + to_core) * 128, 128), 128)
            copy = pltpu.make_async_copy(
                solved_ref.at[:, columns],
                slots.at[part, :, pl.ds(128 * step, 128)],
                sems.at[part, step],
            )
            copy.start()
            copies.append(copy)
    panel_copy = pltpu.make_async_copy(panel_ref, panel_held, small_sems.at[0])
    panel_copy.start()
    hand_copies = []
    if count > 1:
        for i, source in enumerate((extra[0].at[0], extra[1])):
            copy = pltpu.make_async_copy(source, outs[count].at[i], small_sems.at[1 + i])
            copy.start()
            hand_copies.append(copy)
    else:
        add_copy = pltpu.make_async_copy(extra[0], add_held, small_sems.at[1])
        add_copy.start()
        add_copy.wait()
    panel_copy.wait()
    p_high, p_low = halves(-panel_held[...])
    p_both = jnp.concatenate([p_high, p_low], axis=0)
    dot = functools.partial(jnp.dot, preferred_element_type=jnp.float32)
    for part in range(count):
        for two in range(2):
            copies[4 * part + 2 * two].wait()
            copies[4 * part + 2 * two + 1].wait()
            s_high, s_low = halves(slots[part, :, pl.ds(256 * two, 256)])
            wide = dot(p_both, s_high)
            got = wide[64:] + dot(p_high, s_low) + wide[:64]
            for step in range(2 * two, 2 * two + 2):
                block = got[:, 128 * (step % 2) : 128 * (step % 2 + 1)]
                if count == 1:
                    block = block + jnp.where(q == step, add_held[...], 0.0)
                outs[part][step] = block
    for copy in hand_copies:
        copy.wait()


def product(flips, panel, solved, *extra):
    args = (panel, solved) + extra
    count = len(flips)
    shapes = [(4, 64, 128)] * count + ([(2,) + extra[1].shape] if count > 1 else [])
    return pl.pallas_call(
        functools.partial(product_kernel, flips),
        out_shape=[jax.ShapeDtypeStruct(shape, jnp.float32) for shape in shapes],
        in_specs=[pl.BlockSpec(memory_space=pl.ANY)] * len(args),
        out_specs=[pl.BlockSpec(memory_space=pltpu.VMEM)] * len(shapes),
        scratch_shapes=[
            pltpu.VMEM((64, 512), jnp.float32),
            pltpu.VMEM((64, 128), jnp.float32),
            pltpu.VMEM((count, 512, 512), jnp.float32),
            pltpu.SemaphoreType.DMA((count, 4)),
            pltpu.SemaphoreType.DMA((3,)),
        ],
        compiler_params=pltpu.CompilerParams(vmem_limit_bytes=56 << 20),
        cost_estimate=pl.CostEstimate(flops=count * 10**8, bytes_accessed=count << 20, transcendentals=0),
    )(*args)


def gather_plane(block):
    copies = jnp.broadcast_to(block[None], (16,) + block.shape)
    got = lax.all_to_all(copies, ("y", "x"), 0, 0, tiled=True)
    return got.reshape(16 * block.shape[0], block.shape[1])


def on_device(right_side, diag_inverse, coupling, panel, solved):
    zh, q = lax.axis_index("zh"), lax.axis_index("q")
    swap = [(0, 1), (1, 0)]
    flip = lambda m: [(z, z ^ m) for z in range(4)]
    other_half = lambda x: lax.ppermute(x, ("zh",) + LINE, [(z, 15 - z) for z in range(16)])
    take = lambda x, index: lax.dynamic_index_in_dim(x, index, 0, keepdims=False)

    panel = panel.reshape(64, 512)
    *sends, factors = product(((1, 1), (1, 0), (0, 1)), panel, solved, diag_inverse, coupling)
    from_both = lax.ppermute(sends[0], ("b", "core"), flip(3))
    from_pair = lax.ppermute(sends[1], "b", swap)
    from_core = lax.ppermute(sends[2], "core", swap)
    factors = other_half(factors)
    (keep,) = product(((0, 0),), panel, solved, right_side.reshape(64, 128))
    total = keep + from_core + from_pair + from_both
    got = [lax.ppermute(take(total, q ^ m), "q", flip(m)) for m in (1, 2, 3)]
    residual = take(total, q) + got[0] + got[1] + got[2]
    first_half = zh == 0
    residual, factors, first_half = lax.optimization_barrier((residual, factors, first_half))

    def ordered(mine, theirs):
        return jnp.concatenate([jnp.where(first_half, mine, theirs), jnp.where(first_half, theirs, mine)])

    known = gather_plane(residual[:32]).reshape(16, 1, 32, 128)
    known = jnp.concatenate([jnp.where(first_half, known, 0.0), jnp.where(first_half, 0.0, known)], axis=1)
    known = known.reshape(1024, 128)
    parts = jnp.concatenate([mul(diag_inverse[0], known), mul(factors[0], known), residual[32:]])
    across = lax.ppermute(parts, "zh", swap)
    first_mine = parts[:32] + across[32:64]
    first_sol = gather_plane(ordered(first_mine, parts[32:64] + across[:32]))
    mine = residual[32:] - mul(coupling, first_sol)
    theirs = across[64:] - mul(factors[1], first_sol)
    second_mine = mul(diag_inverse[1], gather_plane(ordered(mine, theirs)))
    return jnp.stack([first_mine, second_mine])


def solution(mesh):
    fine = Mesh(mesh.devices.reshape(4, 4, 2, 4, 2, 2), ROWS + COLS)
    return jax.shard_map(
        on_device,
        mesh=fine,
        in_specs=(
            P(None, ROWS, COLS),
            P(None, ROWS, None),
            P(ROWS, None),
            P(None, ROWS, COLS),
            P(COLS, None),
        ),
        out_specs=P(None, ROWS, COLS),
        check_vma=False,
    )
```

```python
import functools

import jax
import jax.numpy as jnp
from jax import lax
from jax.experimental import pallas as pl
from jax.experimental.pallas import tpu as pltpu
from jax.sharding import Mesh, PartitionSpec as P

ROWS = ("y", "x", "zh")
LINE = ("q", "b")
COLS = LINE + ("core",)


def mul(a, b):
    return jnp.dot(a, b, precision=lax.Precision.HIGHEST, preferred_element_type=jnp.float32)


def halves(x):
    high = x.astype(jnp.bfloat16)
    return high, (x - high.astype(jnp.float32)).astype(jnp.bfloat16)


def product_kernel(flips, panel_ref, solved_ref, *rest):
    count = len(flips)
    add_ref = rest[0] if len(rest) > 6 else None
    out_ref = rest[-6]
    panel_held, add_held, slots, sems, small_sems = rest[-5:]
    core, q, b = (lax.axis_index(a) for a in ("core", "q", "b"))
    copies = []
    for part, (flip_b, flip_core) in enumerate(flips):
        to_b = 1 - b if flip_b else b
        to_core = 1 - core if flip_core else core
        for step in range(4):
            columns = pl.ds(pl.multiple_of((4 * step + 2 * to_b + to_core) * 128, 128), 128)
            copy = pltpu.make_async_copy(
                solved_ref.at[:, columns],
                slots.at[part, :, pl.ds(128 * step, 128)],
                sems.at[part, step],
            )
            copy.start()
            copies.append(copy)
    panel_copy = pltpu.make_async_copy(panel_ref, panel_held, small_sems.at[0])
    panel_copy.start()
    if add_ref is not None:
        add_copy = pltpu.make_async_copy(add_ref, add_held, small_sems.at[1])
        add_copy.start()
        add_copy.wait()
    panel_copy.wait()
    p_high, p_low = halves(-panel_held[...])
    p_both = jnp.concatenate([p_high, p_low], axis=0)
    dot = functools.partial(jnp.dot, preferred_element_type=jnp.float32)
    for part in range(count):
        for two in range(2):
            copies[4 * part + 2 * two].wait()
            copies[4 * part + 2 * two + 1].wait()
            s_high, s_low = halves(slots[part, :, pl.ds(256 * two, 256)])
            wide = dot(p_both, s_high)
            got = wide[64:] + dot(p_high, s_low) + wide[:64]
            for step in range(2 * two, 2 * two + 2):
                block = got[:, 128 * (step % 2) : 128 * (step % 2 + 1)]
                if add_ref is not None and flips[part] == (0, 0):
                    block = block + jnp.where(q == step, add_held[...], 0.0)
                out_ref[part, step] = block


def product(flips, panel, solved, add=None):
    args = (panel, solved) + (() if add is None else (add,))
    count = len(flips)
    return pl.pallas_call(
        functools.partial(product_kernel, flips),
        out_shape=jax.ShapeDtypeStruct((count, 4, 64, 128), jnp.float32),
        in_specs=[pl.BlockSpec(memory_space=pl.ANY)] * len(args),
        out_specs=pl.BlockSpec(memory_space=pltpu.VMEM),
        scratch_shapes=[
            pltpu.VMEM((64, 512), jnp.float32),
            pltpu.VMEM((64, 128), jnp.float32),
            pltpu.VMEM((count, 512, 512), jnp.float32),
            pltpu.SemaphoreType.DMA((count, 4)),
            pltpu.SemaphoreType.DMA((2,)),
        ],
        compiler_params=pltpu.CompilerParams(vmem_limit_bytes=56 << 20),
        cost_estimate=pl.CostEstimate(flops=count * 10**8, bytes_accessed=count << 20, transcendentals=0),
    )(*args)


def pair_up(index, mine, theirs):
    first = index == 0
    return jnp.stack([jnp.where(first, mine, theirs), jnp.where(first, theirs, mine)])


def gather_plane(block):
    copies = jnp.broadcast_to(block[None], (16,) + block.shape)
    got = lax.all_to_all(copies, ("y", "x"), 0, 0, tiled=True)
    return got.reshape(16 * block.shape[0], block.shape[1])


def on_device(right_side, diag_inverse, coupling, panel, solved):
    zh, b, core = (lax.axis_index(a) for a in ("zh", "b", "core"))
    swap = [(0, 1), (1, 0)]

    rows = lambda x: lax.dynamic_slice_in_dim(x, 16 * core, 16, 0)
    quarter = jnp.where(b == 1, rows(diag_inverse[0]), rows(coupling))
    quarter = lax.ppermute(quarter, ("zh",) + LINE, [(z, 15 - z) for z in range(16)])

    panel = panel.reshape(64, 512)
    moved = lax.ppermute(product(((1, 1), (0, 1)), panel, solved), "core", swap)
    keep = product(((1, 0), (0, 0)), panel, solved, right_side.reshape(64, 128))
    passed = lax.ppermute(keep[0] + moved[0], "b", swap)
    total = keep[1] + moved[1] + passed
    half = pair_up(b, quarter, lax.ppermute(quarter, "b", swap))
    other = pair_up(core, half, lax.ppermute(half, "core", swap))
    other = other.transpose(1, 0, 2, 3).reshape(2, 32, 1024)
    copies = jnp.broadcast_to(total[None], (2, 4, 64, 128)).reshape(8, 64, 128)
    got_all = lax.all_to_all(copies, ("zh", "q"), 0, 0, tiled=True)
    first_half = zh == 0
    got_all, other, first_half = lax.optimization_barrier((got_all, other, first_half))
    residual = got_all.reshape(2, 4, 2, 32, 128).sum(1)
    first_res = residual[:, 0].reshape(64, 128)
    second_part = residual[:, 1].reshape(64, 128)

    def both(mine, theirs, x):
        a, c = mul(mine, x), mul(theirs, x)
        return jnp.where(first_half, jnp.concatenate([a, c]), jnp.concatenate([c, a])), a

    first_sol, first_mine = both(diag_inverse[0], other[0], gather_plane(first_res))
    cross, _ = both(coupling, other[1], gather_plane(first_sol))
    second_mine = mul(diag_inverse[1], gather_plane(second_part - cross))
    return jnp.stack([first_mine, second_mine])


def solution(mesh):
    fine = Mesh(mesh.devices.reshape(4, 4, 2, 4, 2, 2), ROWS + COLS)
    return jax.shard_map(
        on_device,
        mesh=fine,
        in_specs=(
            P(None, ROWS, COLS),
            P(None, ROWS, None),
            P(ROWS, None),
            P(None, ROWS, COLS),
            P(COLS, None),
        ),
        out_specs=P(None, ROWS, COLS),
        check_vma=False,
    )
```

```python
import functools

import jax
import jax.numpy as jnp
from jax import lax
from jax.experimental import pallas as pl
from jax.experimental.pallas import tpu as pltpu
from jax.sharding import Mesh, PartitionSpec as P

ROWS = ("y", "x", "zh")
LINE = ("q", "b")
COLS = LINE + ("core",)


def mul(a, b):
    return jnp.dot(a, b, precision=lax.Precision.HIGHEST, preferred_element_type=jnp.float32)


def halves(x):
    high = x.astype(jnp.bfloat16)
    return high, (x - high.astype(jnp.float32)).astype(jnp.bfloat16)


def product_kernel(flips, panel_ref, solved_ref, *rest):
    count = len(flips)
    add_ref = rest[0] if len(rest) > 6 else None
    out_ref = rest[-6]
    panel_held, add_held, slots, sems, small_sems = rest[-5:]
    core, q, b = (lax.axis_index(a) for a in ("core", "q", "b"))
    copies = []
    for part, (flip_b, flip_core) in enumerate(flips):
        to_b = 1 - b if flip_b else b
        to_core = 1 - core if flip_core else core
        for step in range(4):
            columns = pl.ds(pl.multiple_of((4 * step + 2 * to_b + to_core) * 128, 128), 128)
            copy = pltpu.make_async_copy(
                solved_ref.at[:, columns],
                slots.at[part, :, pl.ds(128 * step, 128)],
                sems.at[part, step],
            )
            copy.start()
            copies.append(copy)
    panel_copy = pltpu.make_async_copy(panel_ref, panel_held, small_sems.at[0])
    panel_copy.start()
    if add_ref is not None:
        add_copy = pltpu.make_async_copy(add_ref, add_held, small_sems.at[1])
        add_copy.start()
        add_copy.wait()
    panel_copy.wait()
    p_high, p_low = halves(-panel_held[...])
    p_both = jnp.concatenate([p_high, p_low], axis=0)
    dot = functools.partial(jnp.dot, preferred_element_type=jnp.float32)
    for part in range(count):
        for two in range(2):
            copies[4 * part + 2 * two].wait()
            copies[4 * part + 2 * two + 1].wait()
            s_high, s_low = halves(slots[part, :, pl.ds(256 * two, 256)])
            wide = dot(p_both, s_high)
            got = wide[64:] + dot(p_high, s_low) + wide[:64]
            for step in range(2 * two, 2 * two + 2):
                block = got[:, 128 * (step % 2) : 128 * (step % 2 + 1)]
                if add_ref is not None and flips[part] == (0, 0):
                    block = block + jnp.where(q == step, add_held[...], 0.0)
                out_ref[part, step] = block


def product(flips, panel, solved, add=None):
    args = (panel, solved) + (() if add is None else (add,))
    count = len(flips)
    return pl.pallas_call(
        functools.partial(product_kernel, flips),
        out_shape=jax.ShapeDtypeStruct((count, 4, 64, 128), jnp.float32),
        in_specs=[pl.BlockSpec(memory_space=pl.ANY)] * len(args),
        out_specs=pl.BlockSpec(memory_space=pltpu.VMEM),
        scratch_shapes=[
            pltpu.VMEM((64, 512), jnp.float32),
            pltpu.VMEM((64, 128), jnp.float32),
            pltpu.VMEM((count, 512, 512), jnp.float32),
            pltpu.SemaphoreType.DMA((count, 4)),
            pltpu.SemaphoreType.DMA((2,)),
        ],
        compiler_params=pltpu.CompilerParams(vmem_limit_bytes=52 << 20),
        cost_estimate=pl.CostEstimate(flops=count * 10**8, bytes_accessed=count << 20, transcendentals=0),
    )(*args)


def pass_kernel(keep_ref, moved_ref, out_ref):
    out_ref[...] = keep_ref[0] + moved_ref[0]


def spread_kernel(keep_ref, moved_ref, passed_ref, out_ref):
    total = keep_ref[1] + moved_ref[1] + passed_ref[...]
    out_ref[0] = total
    out_ref[1] = total


def in_vmem(kernel, shape, *args):
    vmem = pl.BlockSpec(memory_space=pltpu.VMEM)
    return pl.pallas_call(
        kernel,
        out_shape=jax.ShapeDtypeStruct(shape, jnp.float32),
        in_specs=[vmem] * len(args),
        out_specs=vmem,
        compiler_params=pltpu.CompilerParams(vmem_limit_bytes=4 << 20),
        cost_estimate=pl.CostEstimate(flops=10**6, bytes_accessed=10**6, transcendentals=0),
    )(*args)


def pair_up(index, mine, theirs):
    first = index == 0
    return jnp.stack([jnp.where(first, mine, theirs), jnp.where(first, theirs, mine)])


def gather_plane(block):
    copies = jnp.broadcast_to(block[None], (16,) + block.shape)
    got = lax.all_to_all(copies, ("y", "x"), 0, 0, tiled=True)
    return got.reshape(16 * block.shape[0], block.shape[1])


def on_device(right_side, diag_inverse, coupling, panel, solved):
    zh, b, core = (lax.axis_index(a) for a in ("zh", "b", "core"))
    swap = [(0, 1), (1, 0)]

    rows = lambda x: lax.dynamic_slice_in_dim(x, 16 * core, 16, 0)
    quarter = jnp.where(b == 1, rows(diag_inverse[0]), rows(coupling))
    quarter = lax.ppermute(quarter, ("zh",) + LINE, [(z, 15 - z) for z in range(16)])

    panel = panel.reshape(64, 512)
    moved = lax.ppermute(product(((1, 1), (0, 1)), panel, solved), "core", swap)
    keep = product(((1, 0), (0, 0)), panel, solved, right_side.reshape(64, 128))
    passed = lax.ppermute(in_vmem(pass_kernel, (4, 64, 128), keep, moved), "b", swap)
    copies = in_vmem(spread_kernel, (2, 4, 64, 128), keep, moved, passed).reshape(8, 64, 128)
    half = pair_up(core, quarter, lax.ppermute(quarter, "core", swap))
    other = pair_up(b, half, lax.ppermute(half, "b", swap)).reshape(2, 32, 1024)
    got_all = lax.all_to_all(copies, ("zh", "q"), 0, 0, tiled=True)
    first_half = zh == 0
    got_all, other, first_half = lax.optimization_barrier((got_all, other, first_half))
    residual = got_all.reshape(2, 4, 2, 32, 128).sum(1)
    first_res = residual[:, 0].reshape(64, 128)
    second_part = residual[:, 1].reshape(64, 128)

    def both(mine, theirs, x):
        a, c = mul(mine, x), mul(theirs, x)
        return jnp.where(first_half, jnp.concatenate([a, c]), jnp.concatenate([c, a])), a

    first_sol, first_mine = both(diag_inverse[0], other[0], gather_plane(first_res))
    cross, _ = both(coupling, other[1], gather_plane(first_sol))
    second_mine = mul(diag_inverse[1], gather_plane(second_part - cross))
    return jnp.stack([first_mine, second_mine])


def solution(mesh):
    fine = Mesh(mesh.devices.reshape(4, 4, 2, 4, 2, 2), ROWS + COLS)
    return jax.shard_map(
        on_device,
        mesh=fine,
        in_specs=(
            P(None, ROWS, COLS),
            P(None, ROWS, None),
            P(ROWS, None),
            P(None, ROWS, COLS),
            P(COLS, None),
        ),
        out_specs=P(None, ROWS, COLS),
        check_vma=False,
    )
```

```python
import functools

import jax
import jax.numpy as jnp
from jax import lax
from jax.experimental import pallas as pl
from jax.experimental.pallas import tpu as pltpu
from jax.sharding import Mesh, PartitionSpec as P

ROWS = ("y", "x", "zh")
LINE = ("q", "b")
COLS = LINE + ("core",)


def halves(x):
    high = x.astype(jnp.bfloat16)
    return high, (x - high.astype(jnp.float32)).astype(jnp.bfloat16)


def product_kernel(flips, panel_ref, solved_ref, *rest):
    count = len(flips)
    add_ref = rest[0] if len(rest) > 6 else None
    out_ref = rest[-6]
    panel_held, add_held, slots, sems, small_sems = rest[-5:]
    core, q, b = (lax.axis_index(a) for a in ("core", "q", "b"))
    copies = []
    for part, (flip_b, flip_core) in enumerate(flips):
        to_b = 1 - b if flip_b else b
        to_core = 1 - core if flip_core else core
        for step in range(4):
            columns = pl.ds(pl.multiple_of((4 * step + 2 * to_b + to_core) * 128, 128), 128)
            copy = pltpu.make_async_copy(
                solved_ref.at[:, columns],
                slots.at[part, :, pl.ds(128 * step, 128)],
                sems.at[part, step],
            )
            copy.start()
            copies.append(copy)
    panel_copy = pltpu.make_async_copy(panel_ref, panel_held, small_sems.at[0])
    panel_copy.start()
    if add_ref is not None:
        add_copy = pltpu.make_async_copy(add_ref, add_held, small_sems.at[1])
        add_copy.start()
        add_copy.wait()
    panel_copy.wait()
    p_high, p_low = halves(-panel_held[...])
    p_both = jnp.concatenate([p_high, p_low], axis=0)
    dot = functools.partial(jnp.dot, preferred_element_type=jnp.float32)
    for part in range(count):
        for two in range(2):
            copies[4 * part + 2 * two].wait()
            copies[4 * part + 2 * two + 1].wait()
            s_high, s_low = halves(slots[part, :, pl.ds(256 * two, 256)])
            wide = dot(p_both, s_high)
            got = wide[64:] + dot(p_high, s_low) + wide[:64]
            for step in range(2 * two, 2 * two + 2):
                block = got[:, 128 * (step % 2) : 128 * (step % 2 + 1)]
                if add_ref is not None and flips[part] == (0, 0):
                    block = block + jnp.where(q == step, add_held[...], 0.0)
                out_ref[part, step] = block


def product(flips, panel, solved, add=None):
    args = (panel, solved) + (() if add is None else (add,))
    count = len(flips)
    return pl.pallas_call(
        functools.partial(product_kernel, flips),
        out_shape=jax.ShapeDtypeStruct((count, 4, 64, 128), jnp.float32),
        in_specs=[pl.BlockSpec(memory_space=pl.ANY)] * len(args),
        out_specs=pl.BlockSpec(memory_space=pltpu.VMEM),
        scratch_shapes=[
            pltpu.VMEM((64, 512), jnp.float32),
            pltpu.VMEM((64, 128), jnp.float32),
            pltpu.VMEM((count, 512, 512), jnp.float32),
            pltpu.SemaphoreType.DMA((count, 4)),
            pltpu.SemaphoreType.DMA((2,)),
        ],
        compiler_params=pltpu.CompilerParams(vmem_limit_bytes=52 << 20),
        cost_estimate=pl.CostEstimate(flops=count * 10**8, bytes_accessed=count << 20, transcendentals=0),
    )(*args)


def pass_kernel(keep_ref, moved_ref, out_ref):
    out_ref[...] = keep_ref[0] + moved_ref[0]


def spread_kernel(keep_ref, moved_ref, passed_ref, out_ref):
    total = keep_ref[1] + moved_ref[1] + passed_ref[...]
    out_ref[0] = total
    out_ref[1] = total


def times(factor, x):
    f_high, f_low = halves(factor)
    x_high, x_low = halves(x)
    dot = functools.partial(jnp.dot, preferred_element_type=jnp.float32)
    wide = dot(jnp.concatenate([f_high, f_low], axis=0), x_high)
    rows = factor.shape[0]
    return wide[rows:] + dot(f_high, x_low) + wide[:rows]


def rows_kernel(step, mine_ref, theirs_ref, x_ref, *rest):
    out_ref = rest[-1]
    zh = lax.axis_index("zh")
    got = times(jnp.concatenate([mine_ref[0], theirs_ref[step]], axis=0), x_ref[...])
    got = jnp.where(zh == 0, got, jnp.concatenate([got[32:], got[:32]], axis=0))
    out_ref[...] = rest[0][...] - got if len(rest) == 2 else got


def last_kernel(factor_ref, x_ref, first_ref, out_ref):
    zh = lax.axis_index("zh")
    out_ref[0] = jnp.where(zh == 0, first_ref[:32], first_ref[32:])
    out_ref[1] = times(factor_ref[1], x_ref[...])


def in_vmem(kernel, shape, *args):
    vmem = pl.BlockSpec(memory_space=pltpu.VMEM)
    return pl.pallas_call(
        kernel,
        out_shape=jax.ShapeDtypeStruct(shape, jnp.float32),
        in_specs=[vmem] * len(args),
        out_specs=vmem,
        compiler_params=pltpu.CompilerParams(vmem_limit_bytes=8 << 20),
        cost_estimate=pl.CostEstimate(flops=10**6, bytes_accessed=10**6, transcendentals=0),
    )(*args)


def pair_up(index, mine, theirs):
    first = index == 0
    return jnp.stack([jnp.where(first, mine, theirs), jnp.where(first, theirs, mine)])


def gather_plane(block):
    copies = jnp.broadcast_to(block[None], (16,) + block.shape)
    got = lax.all_to_all(copies, ("y", "x"), 0, 0, tiled=True)
    return got.reshape(16 * block.shape[0], block.shape[1])


def on_device(right_side, diag_inverse, coupling, panel, solved):
    b, core = (lax.axis_index(a) for a in ("b", "core"))
    swap = [(0, 1), (1, 0)]

    rows = lambda x: lax.dynamic_slice_in_dim(x, 16 * core, 16, 0)
    quarter = jnp.where(b == 1, rows(diag_inverse[0]), rows(coupling))
    quarter = lax.ppermute(quarter, ("zh",) + LINE, [(z, 15 - z) for z in range(16)])

    panel = panel.reshape(64, 512)
    moved = lax.ppermute(product(((1, 1), (0, 1)), panel, solved), "core", swap)
    keep = product(((1, 0), (0, 0)), panel, solved, right_side.reshape(64, 128))
    passed = lax.ppermute(in_vmem(pass_kernel, (4, 64, 128), keep, moved), "b", swap)
    copies = in_vmem(spread_kernel, (2, 4, 64, 128), keep, moved, passed).reshape(8, 64, 128)
    half = pair_up(core, quarter, lax.ppermute(quarter, "core", swap))
    other = pair_up(b, half, lax.ppermute(half, "b", swap)).reshape(2, 32, 1024)
    got_all = lax.all_to_all(copies, ("zh", "q"), 0, 0, tiled=True)
    got_all, other = lax.optimization_barrier((got_all, other))
    residual = got_all.reshape(2, 4, 2, 32, 128).sum(1)
    first_res = residual[:, 0].reshape(64, 128)
    second_part = residual[:, 1].reshape(64, 128)

    first_rows, second_rows = (functools.partial(rows_kernel, step) for step in range(2))
    first_sol = in_vmem(first_rows, (64, 128), diag_inverse, other, gather_plane(first_res))
    second_res = in_vmem(
        second_rows, (64, 128), coupling[None], other, gather_plane(first_sol), second_part
    )
    return in_vmem(last_kernel, (2, 32, 128), diag_inverse, gather_plane(second_res), first_sol)


def solution(mesh):
    fine = Mesh(mesh.devices.reshape(4, 4, 2, 4, 2, 2), ROWS + COLS)
    return jax.shard_map(
        on_device,
        mesh=fine,
        in_specs=(
            P(None, ROWS, COLS),
            P(None, ROWS, None),
            P(ROWS, None),
            P(None, ROWS, COLS),
            P(COLS, None),
        ),
        out_specs=P(None, ROWS, COLS),
        check_vma=False,
    )
```

```python
import functools

import jax
import jax.numpy as jnp
from jax import lax
from jax.experimental import pallas as pl
from jax.experimental.pallas import tpu as pltpu
from jax.sharding import Mesh, PartitionSpec as P

ROWS = ("y", "x", "zh")
LINE = ("q", "b")
COLS = LINE + ("core",)


def halves(x):
    high = x.astype(jnp.bfloat16)
    return high, (x - high.astype(jnp.float32)).astype(jnp.bfloat16)


def product_kernel(flips, panel_ref, solved_ref, *rest):
    count = len(flips)
    add_ref = rest[0] if len(rest) > 6 else None
    out_ref = rest[-6]
    panel_held, add_held, slots, sems, small_sems = rest[-5:]
    core, q, b = (lax.axis_index(a) for a in ("core", "q", "b"))
    copies = []
    for part, (flip_b, flip_core) in enumerate(flips):
        to_b = 1 - b if flip_b else b
        to_core = 1 - core if flip_core else core
        for step in range(4):
            columns = pl.ds(pl.multiple_of((4 * step + 2 * to_b + to_core) * 128, 128), 128)
            copy = pltpu.make_async_copy(
                solved_ref.at[:, columns],
                slots.at[part, :, pl.ds(128 * step, 128)],
                sems.at[part, step],
            )
            copy.start()
            copies.append(copy)
    panel_copy = pltpu.make_async_copy(panel_ref, panel_held, small_sems.at[0])
    panel_copy.start()
    if add_ref is not None:
        add_copy = pltpu.make_async_copy(add_ref, add_held, small_sems.at[1])
        add_copy.start()
        add_copy.wait()
    panel_copy.wait()
    p_high, p_low = halves(-panel_held[...])
    p_both = jnp.concatenate([p_high, p_low], axis=0)
    dot = functools.partial(jnp.dot, preferred_element_type=jnp.float32)
    for part in range(count):
        for two in range(2):
            copies[4 * part + 2 * two].wait()
            copies[4 * part + 2 * two + 1].wait()
            s_high, s_low = halves(slots[part, :, pl.ds(256 * two, 256)])
            wide = dot(p_both, s_high)
            got = wide[64:] + dot(p_high, s_low) + wide[:64]
            for step in range(2 * two, 2 * two + 2):
                block = got[:, 128 * (step % 2) : 128 * (step % 2 + 1)]
                if add_ref is not None and flips[part] == (0, 0):
                    block = block + jnp.where(q == step, add_held[...], 0.0)
                out_ref[part, step] = block


def product(flips, panel, solved, add=None):
    args = (panel, solved) + (() if add is None else (add,))
    count = len(flips)
    return pl.pallas_call(
        functools.partial(product_kernel, flips),
        out_shape=jax.ShapeDtypeStruct((count, 4, 64, 128), jnp.float32),
        in_specs=[pl.BlockSpec(memory_space=pl.ANY)] * len(args),
        out_specs=pl.BlockSpec(memory_space=pltpu.VMEM),
        scratch_shapes=[
            pltpu.VMEM((64, 512), jnp.float32),
            pltpu.VMEM((64, 128), jnp.float32),
            pltpu.VMEM((count, 512, 512), jnp.float32),
            pltpu.SemaphoreType.DMA((count, 4)),
            pltpu.SemaphoreType.DMA((2,)),
        ],
        compiler_params=pltpu.CompilerParams(vmem_limit_bytes=52 << 20),
        cost_estimate=pl.CostEstimate(flops=count * 10**8, bytes_accessed=count << 20, transcendentals=0),
    )(*args)


def pass_kernel(keep_ref, moved_ref, out_ref):
    out_ref[...] = keep_ref[0] + moved_ref[0]


def spread_kernel(keep_ref, moved_ref, passed_ref, out_ref):
    total = keep_ref[1] + moved_ref[1] + passed_ref[...]
    out_ref[:, 0] = total
    out_ref[:, 1] = total


def times(factor, blocks_ref):
    x = jnp.concatenate([blocks_ref[4 * x + y] for y in range(4) for x in range(4)], axis=0)
    f_high, f_low = halves(factor)
    x_high, x_low = halves(x)
    dot = functools.partial(jnp.dot, preferred_element_type=jnp.float32)
    wide = dot(jnp.concatenate([f_high, f_low], axis=0), x_high)
    rows = factor.shape[0]
    return wide[rows:] + dot(f_high, x_low) + wide[:rows]


def rows_kernel(step, mine_ref, theirs_ref, x_ref, *rest):
    out_ref = rest[-1]
    zh = lax.axis_index("zh")
    got = times(jnp.concatenate([mine_ref[0], theirs_ref[step]], axis=0), x_ref)
    got = jnp.where(zh == 0, got, jnp.concatenate([got[32:], got[:32]], axis=0))
    out_ref[...] = rest[0][...] - got if len(rest) == 2 else got


def last_kernel(factor_ref, x_ref, first_ref, out_ref):
    zh = lax.axis_index("zh")
    out_ref[0] = jnp.where(zh == 0, first_ref[:32], first_ref[32:])
    out_ref[1] = times(factor_ref[1], x_ref)


def in_vmem(kernel, shape, *args):
    vmem = pl.BlockSpec(memory_space=pltpu.VMEM)
    return pl.pallas_call(
        kernel,
        out_shape=jax.ShapeDtypeStruct(shape, jnp.float32),
        in_specs=[vmem] * len(args),
        out_specs=vmem,
        compiler_params=pltpu.CompilerParams(vmem_limit_bytes=8 << 20),
        cost_estimate=pl.CostEstimate(flops=10**6, bytes_accessed=10**6, transcendentals=0),
    )(*args)


def pair_up(index, mine, theirs):
    first = index == 0
    return jnp.stack([jnp.where(first, mine, theirs), jnp.where(first, theirs, mine)])


def gather_plane(block):
    copies = jnp.broadcast_to(block[None], (16,) + block.shape)
    return lax.all_to_all(copies, ("x", "y"), 0, 0, tiled=True)


def on_device(right_side, diag_inverse, coupling, panel, solved):
    b, core = (lax.axis_index(a) for a in ("b", "core"))
    swap = [(0, 1), (1, 0)]

    rows = lambda x: lax.dynamic_slice_in_dim(x, 16 * core, 16, 0)
    quarter = jnp.where(b == 1, rows(diag_inverse[0]), rows(coupling))
    quarter = lax.ppermute(quarter, ("zh",) + LINE, [(z, 15 - z) for z in range(16)])

    panel = panel.reshape(64, 512)
    moved = lax.ppermute(product(((1, 1), (0, 1)), panel, solved), "core", swap)
    keep = product(((1, 0), (0, 0)), panel, solved, right_side.reshape(64, 128))
    passed = lax.ppermute(in_vmem(pass_kernel, (4, 64, 128), keep, moved), "b", swap)
    copies = in_vmem(spread_kernel, (4, 2, 64, 128), keep, moved, passed).reshape(8, 64, 128)
    half = pair_up(core, quarter, lax.ppermute(quarter, "core", swap))
    other = pair_up(b, half, lax.ppermute(half, "b", swap)).reshape(2, 32, 1024)
    got_all = lax.all_to_all(copies, ("q", "zh"), 0, 0, tiled=True)
    got_all, other = lax.optimization_barrier((got_all, other))
    residual = got_all.reshape(4, 2, 2, 32, 128).sum(0)
    first_res = residual[:, 0].reshape(64, 128)
    second_part = residual[:, 1].reshape(64, 128)

    first_rows, second_rows = (functools.partial(rows_kernel, step) for step in range(2))
    first_sol = in_vmem(first_rows, (64, 128), diag_inverse, other, gather_plane(first_res))
    second_res = in_vmem(
        second_rows, (64, 128), coupling[None], other, gather_plane(first_sol), second_part
    )
    return in_vmem(last_kernel, (2, 32, 128), diag_inverse, gather_plane(second_res), first_sol)


def solution(mesh):
    fine = Mesh(mesh.devices.reshape(4, 4, 2, 4, 2, 2), ROWS + COLS)
    return jax.shard_map(
        on_device,
        mesh=fine,
        in_specs=(
            P(None, ROWS, COLS),
            P(None, ROWS, None),
            P(ROWS, None),
            P(None, ROWS, COLS),
            P(COLS, None),
        ),
        out_specs=P(None, ROWS, COLS),
        check_vma=False,
    )
```

```python
import functools

import jax
import jax.numpy as jnp
from jax import lax
from jax.experimental import pallas as pl
from jax.experimental.pallas import tpu as pltpu
from jax.sharding import Mesh, PartitionSpec as P

ROWS = ("y", "x", "zh")
LINE = ("q", "b")
COLS = LINE + ("core",)


def halves(x):
    high = x.astype(jnp.bfloat16)
    return high, (x - high.astype(jnp.float32)).astype(jnp.bfloat16)


def product_kernel(flips, panel_ref, solved_ref, *rest):
    count = len(flips)
    add_ref = rest[0] if len(rest) > 6 else None
    out_ref = rest[-6]
    panel_held, add_held, slots, sems, small_sems = rest[-5:]
    core, q, b = (lax.axis_index(a) for a in ("core", "q", "b"))
    copies = []
    for part, (flip_b, flip_core) in enumerate(flips):
        to_b = 1 - b if flip_b else b
        to_core = 1 - core if flip_core else core
        for step in range(4):
            columns = pl.ds(pl.multiple_of((4 * step + 2 * to_b + to_core) * 128, 128), 128)
            copy = pltpu.make_async_copy(
                solved_ref.at[:, columns],
                slots.at[part, :, pl.ds(128 * step, 128)],
                sems.at[part, step],
            )
            copy.start()
            copies.append(copy)
    panel_copy = pltpu.make_async_copy(panel_ref, panel_held, small_sems.at[0])
    panel_copy.start()
    if add_ref is not None:
        add_copy = pltpu.make_async_copy(add_ref, add_held, small_sems.at[1])
        add_copy.start()
        add_copy.wait()
    panel_copy.wait()
    p_high, p_low = halves(-panel_held[...])
    p_both = jnp.concatenate([p_high, p_low], axis=0)
    dot = functools.partial(jnp.dot, preferred_element_type=jnp.float32)
    for part in range(count):
        for two in range(2):
            copies[4 * part + 2 * two].wait()
            copies[4 * part + 2 * two + 1].wait()
            s_high, s_low = halves(slots[part, :, pl.ds(256 * two, 256)])
            wide = dot(p_both, s_high)
            got = wide[64:] + dot(p_high, s_low) + wide[:64]
            for step in range(2 * two, 2 * two + 2):
                block = got[:, 128 * (step % 2) : 128 * (step % 2 + 1)]
                if add_ref is not None and flips[part] == (0, 0):
                    block = block + jnp.where(q == step, add_held[...], 0.0)
                out_ref[part, step] = block


def product(flips, panel, solved, add=None):
    args = (panel, solved) + (() if add is None else (add,))
    count = len(flips)
    return pl.pallas_call(
        functools.partial(product_kernel, flips),
        out_shape=jax.ShapeDtypeStruct((count, 4, 64, 128), jnp.float32),
        in_specs=[pl.BlockSpec(memory_space=pl.ANY)] * len(args),
        out_specs=pl.BlockSpec(memory_space=pltpu.VMEM),
        scratch_shapes=[
            pltpu.VMEM((64, 512), jnp.float32),
            pltpu.VMEM((64, 128), jnp.float32),
            pltpu.VMEM((count, 512, 512), jnp.float32),
            pltpu.SemaphoreType.DMA((count, 4)),
            pltpu.SemaphoreType.DMA((2,)),
        ],
        compiler_params=pltpu.CompilerParams(vmem_limit_bytes=52 << 20),
        cost_estimate=pl.CostEstimate(flops=count * 10**8, bytes_accessed=count << 20, transcendentals=0),
    )(*args)


def pass_kernel(keep_ref, moved_ref, out_ref):
    out_ref[...] = keep_ref[0] + moved_ref[0]


def spread_kernel(keep_ref, moved_ref, passed_ref, out_ref):
    total = keep_ref[1] + moved_ref[1] + passed_ref[...]
    out_ref[:, 0] = total
    out_ref[:, 1] = total


def times(factor, blocks_ref):
    x = blocks_ref[...].reshape(1024, 128)
    f_high, f_low = halves(factor)
    x_high, x_low = halves(x)
    dot = functools.partial(jnp.dot, preferred_element_type=jnp.float32)
    wide = dot(jnp.concatenate([f_high, f_low], axis=0), x_high)
    rows = factor.shape[0]
    return wide[rows:] + dot(f_high, x_low) + wide[:rows]


def rows_kernel(step, mine_ref, theirs_ref, x_ref, *rest):
    out_ref = rest[-1]
    zh = lax.axis_index("zh")
    got = times(jnp.concatenate([mine_ref[0], theirs_ref[step]], axis=0), x_ref)
    got = jnp.where(zh == 0, got, jnp.concatenate([got[32:], got[:32]], axis=0))
    out_ref[...] = rest[0][...] - got if len(rest) == 2 else got


def last_kernel(factor_ref, x_ref, first_ref, out_ref):
    zh = lax.axis_index("zh")
    out_ref[0] = jnp.where(zh == 0, first_ref[:32], first_ref[32:])
    out_ref[1] = times(factor_ref[1], x_ref)


def in_vmem(kernel, shape, *args):
    vmem = pl.BlockSpec(memory_space=pltpu.VMEM)
    return pl.pallas_call(
        kernel,
        out_shape=jax.ShapeDtypeStruct(shape, jnp.float32),
        in_specs=[vmem] * len(args),
        out_specs=vmem,
        compiler_params=pltpu.CompilerParams(vmem_limit_bytes=8 << 20),
        cost_estimate=pl.CostEstimate(flops=10**6, bytes_accessed=10**6, transcendentals=0),
    )(*args)


def pair_up(index, mine, theirs):
    first = index == 0
    return jnp.stack([jnp.where(first, mine, theirs), jnp.where(first, theirs, mine)])


def gather_plane(block):
    copies = jnp.broadcast_to(block[None], (16,) + block.shape)
    return lax.all_to_all(copies, ("y", "x"), 0, 0, tiled=True)


def on_device(right_side, diag_inverse, coupling, panel, solved):
    b, core = (lax.axis_index(a) for a in ("b", "core"))
    swap = [(0, 1), (1, 0)]

    rows = lambda x: lax.dynamic_slice_in_dim(x, 16 * core, 16, 0)
    quarter = jnp.where(b == 1, rows(diag_inverse[0]), rows(coupling))
    quarter = lax.ppermute(quarter, ("zh",) + LINE, [(z, 15 - z) for z in range(16)])

    panel = panel.reshape(64, 512)
    moved = lax.ppermute(product(((1, 1), (0, 1)), panel, solved), "core", swap)
    keep = product(((1, 0), (0, 0)), panel, solved, right_side.reshape(64, 128))
    passed = lax.ppermute(in_vmem(pass_kernel, (4, 64, 128), keep, moved), "b", swap)
    copies = in_vmem(spread_kernel, (4, 2, 64, 128), keep, moved, passed).reshape(8, 64, 128)
    half = pair_up(core, quarter, lax.ppermute(quarter, "core", swap))
    other = pair_up(b, half, lax.ppermute(half, "b", swap)).reshape(2, 32, 1024)
    got_all = lax.all_to_all(copies, ("q", "zh"), 0, 0, tiled=True)
    got_all, other = lax.optimization_barrier((got_all, other))
    residual = got_all.reshape(4, 2, 2, 32, 128).sum(0)
    first_res = residual[:, 0].reshape(64, 128)
    second_part = residual[:, 1].reshape(64, 128)

    first_rows, second_rows = (functools.partial(rows_kernel, step) for step in range(2))
    first_sol = in_vmem(first_rows, (64, 128), diag_inverse, other, gather_plane(first_res))
    second_res = in_vmem(
        second_rows, (64, 128), coupling[None], other, gather_plane(first_sol), second_part
    )
    return in_vmem(last_kernel, (2, 32, 128), diag_inverse, gather_plane(second_res), first_sol)


def solution(mesh):
    fine = Mesh(mesh.devices.reshape(4, 4, 2, 4, 2, 2), ROWS + COLS)
    return jax.shard_map(
        on_device,
        mesh=fine,
        in_specs=(
            P(None, ROWS, COLS),
            P(None, ROWS, None),
            P(ROWS, None),
            P(None, ROWS, COLS),
            P(COLS, None),
        ),
        out_specs=P(None, ROWS, COLS),
        check_vma=False,
    )
```

```python
import functools

import jax
import jax.numpy as jnp
from jax import lax
from jax.experimental import pallas as pl
from jax.experimental.pallas import tpu as pltpu
from jax.sharding import Mesh, PartitionSpec as P

ROWS = ("y", "x", "zh")
LINE = ("q", "b")
COLS = LINE + ("core",)


def halves(x):
    high = x.astype(jnp.bfloat16)
    return high, (x - high.astype(jnp.float32)).astype(jnp.bfloat16)


def product_kernel(flips, panel_ref, solved_ref, *rest):
    count = len(flips)
    add_ref = rest[0] if len(rest) > 6 else None
    out_ref = rest[-6]
    panel_held, add_held, slots, sems, small_sems = rest[-5:]
    core, q, b = (lax.axis_index(a) for a in ("core", "q", "b"))
    copies = []
    for part, (flip_b, flip_core) in enumerate(flips):
        to_b = 1 - b if flip_b else b
        to_core = 1 - core if flip_core else core
        for step in range(4):
            columns = pl.ds(pl.multiple_of((4 * step + 2 * to_b + to_core) * 128, 128), 128)
            copy = pltpu.make_async_copy(
                solved_ref.at[:, columns],
                slots.at[part, :, pl.ds(128 * step, 128)],
                sems.at[part, step],
            )
            copy.start()
            copies.append(copy)
    panel_copy = pltpu.make_async_copy(panel_ref, panel_held, small_sems.at[0])
    panel_copy.start()
    if add_ref is not None:
        add_copy = pltpu.make_async_copy(add_ref, add_held, small_sems.at[1])
        add_copy.start()
        add_copy.wait()
    panel_copy.wait()
    p_high, p_low = halves(-panel_held[...])
    p_both = jnp.concatenate([p_high, p_low], axis=0)
    dot = functools.partial(jnp.dot, preferred_element_type=jnp.float32)
    for part in range(count):
        for two in range(2):
            copies[4 * part + 2 * two].wait()
            copies[4 * part + 2 * two + 1].wait()
            s_high, s_low = halves(slots[part, :, pl.ds(256 * two, 256)])
            wide = dot(p_both, s_high)
            got = wide[64:] + dot(p_high, s_low) + wide[:64]
            for step in range(2 * two, 2 * two + 2):
                block = got[:, 128 * (step % 2) : 128 * (step % 2 + 1)]
                if add_ref is not None and flips[part] == (0, 0):
                    block = block + jnp.where(q == step, add_held[...], 0.0)
                out_ref[part, step] = block


def product(flips, panel, solved, add=None):
    args = (panel, solved) + (() if add is None else (add,))
    count = len(flips)
    return pl.pallas_call(
        functools.partial(product_kernel, flips),
        out_shape=jax.ShapeDtypeStruct((count, 4, 64, 128), jnp.float32),
        in_specs=[pl.BlockSpec(memory_space=pl.ANY)] * len(args),
        out_specs=pl.BlockSpec(memory_space=pltpu.VMEM),
        scratch_shapes=[
            pltpu.VMEM((64, 512), jnp.float32),
            pltpu.VMEM((64, 128), jnp.float32),
            pltpu.VMEM((count, 512, 512), jnp.float32),
            pltpu.SemaphoreType.DMA((count, 4)),
            pltpu.SemaphoreType.DMA((2,)),
        ],
        compiler_params=pltpu.CompilerParams(vmem_limit_bytes=52 << 20),
        cost_estimate=pl.CostEstimate(flops=count * 10**8, bytes_accessed=count << 20, transcendentals=0),
    )(*args)


def pass_kernel(keep_ref, moved_ref, out_ref):
    out_ref[...] = keep_ref[0] + moved_ref[0]


def spread_kernel(keep_ref, moved_ref, passed_ref, out_ref):
    total = keep_ref[1] + moved_ref[1] + passed_ref[...]
    out_ref[:, 0] = total
    out_ref[:, 1] = total


def times(factor, blocks_ref):
    x = blocks_ref[...].reshape(1024, 128)
    f_high, f_low = halves(factor)
    x_high, x_low = halves(x)
    dot = functools.partial(jnp.dot, preferred_element_type=jnp.float32)
    wide = dot(jnp.concatenate([f_high, f_low], axis=0), x_high)
    rows = factor.shape[0]
    return wide[rows:] + dot(f_high, x_low) + wide[:rows]


def rows_kernel(step, mine_ref, theirs_ref, x_ref, *rest):
    out_ref = rest[-1]
    zh = lax.axis_index("zh")
    got = times(jnp.concatenate([mine_ref[0], theirs_ref[step]], axis=0), x_ref)
    got = jnp.where(zh == 0, got, jnp.concatenate([got[32:], got[:32]], axis=0))
    out_ref[...] = rest[0][...] - got if len(rest) == 2 else got


def last_kernel(factor_ref, x_ref, first_ref, out_ref):
    zh = lax.axis_index("zh")
    out_ref[0] = jnp.where(zh == 0, first_ref[:32], first_ref[32:])
    out_ref[1] = times(factor_ref[1], x_ref)


def in_vmem(kernel, shape, *args):
    vmem = pl.BlockSpec(memory_space=pltpu.VMEM)
    return pl.pallas_call(
        kernel,
        out_shape=jax.ShapeDtypeStruct(shape, jnp.float32),
        in_specs=[vmem] * len(args),
        out_specs=vmem,
        compiler_params=pltpu.CompilerParams(vmem_limit_bytes=8 << 20),
        cost_estimate=pl.CostEstimate(flops=10**6, bytes_accessed=10**6, transcendentals=0),
    )(*args)


def pair_up(index, mine, theirs):
    first = index == 0
    return jnp.stack([jnp.where(first, mine, theirs), jnp.where(first, theirs, mine)])


def gather_plane(block):
    copies = jnp.broadcast_to(block[None], (16,) + block.shape)
    return lax.all_to_all(copies, ("y", "x"), 0, 0, tiled=True)


def on_device(right_side, diag_inverse, coupling, panel, solved):
    b, core = (lax.axis_index(a) for a in ("b", "core"))
    swap = [(0, 1), (1, 0)]

    rows = lambda x: lax.dynamic_slice_in_dim(x, 16 * core, 16, 0)
    quarter = jnp.where(b == 1, rows(diag_inverse[0]), rows(coupling))
    quarter = lax.ppermute(quarter, ("zh",) + LINE, [(z, 15 - z) for z in range(16)])

    panel = panel.reshape(64, 512)
    moved = lax.ppermute(product(((1, 1), (0, 1)), panel, solved), "core", swap)
    keep = product(((1, 0), (0, 0)), panel, solved, right_side.reshape(64, 128))
    passed = lax.ppermute(in_vmem(pass_kernel, (4, 64, 128), keep, moved), "b", swap)
    copies = in_vmem(spread_kernel, (4, 2, 64, 128), keep, moved, passed).reshape(8, 64, 128)
    half = pair_up(b, quarter, lax.ppermute(quarter, "b", swap))
    other = pair_up(core, half, lax.ppermute(half, "core", swap))
    other = other.transpose(1, 0, 2, 3).reshape(2, 32, 1024)
    got_all = lax.all_to_all(copies, ("q", "zh"), 0, 0, tiled=True)
    got_all, other = lax.optimization_barrier((got_all, other))
    residual = got_all.reshape(4, 2, 2, 32, 128).sum(0)
    first_res = residual[:, 0].reshape(64, 128)
    second_part = residual[:, 1].reshape(64, 128)

    first_rows, second_rows = (functools.partial(rows_kernel, step) for step in range(2))
    first_sol = in_vmem(first_rows, (64, 128), diag_inverse, other, gather_plane(first_res))
    second_res = in_vmem(
        second_rows, (64, 128), coupling[None], other, gather_plane(first_sol), second_part
    )
    return in_vmem(last_kernel, (2, 32, 128), diag_inverse, gather_plane(second_res), first_sol)


def solution(mesh):
    fine = Mesh(mesh.devices.reshape(4, 4, 2, 4, 2, 2), ROWS + COLS)
    return jax.shard_map(
        on_device,
        mesh=fine,
        in_specs=(
            P(None, ROWS, COLS),
            P(None, ROWS, None),
            P(ROWS, None),
            P(None, ROWS, COLS),
            P(COLS, None),
        ),
        out_specs=P(None, ROWS, COLS),
        check_vma=False,
    )
```

```python
import functools

import jax
import jax.numpy as jnp
from jax import lax
from jax.experimental import pallas as pl
from jax.experimental.pallas import tpu as pltpu
from jax.sharding import Mesh, PartitionSpec as P

ROWS = ("y", "x", "zh")
LINE = ("q", "b")
COLS = LINE + ("core",)


def halves(x):
    high = x.astype(jnp.bfloat16)
    return high, (x - high.astype(jnp.float32)).astype(jnp.bfloat16)


def product_kernel(flips, panel_ref, solved_ref, *rest):
    count = len(flips)
    add_ref = rest[0] if len(rest) > 6 else None
    out_ref = rest[-6]
    panel_held, add_held, slots, sems, small_sems = rest[-5:]
    core, q, b = (lax.axis_index(a) for a in ("core", "q", "b"))
    copies = []
    for part, (flip_b, flip_core) in enumerate(flips):
        to_b = 1 - b if flip_b else b
        to_core = 1 - core if flip_core else core
        for step in range(4):
            columns = pl.ds(pl.multiple_of((4 * step + 2 * to_b + to_core) * 128, 128), 128)
            copy = pltpu.make_async_copy(
                solved_ref.at[:, columns],
                slots.at[part, :, pl.ds(128 * step, 128)],
                sems.at[part, step],
            )
            copy.start()
            copies.append(copy)
    panel_copy = pltpu.make_async_copy(panel_ref, panel_held, small_sems.at[0])
    panel_copy.start()
    if add_ref is not None:
        add_copy = pltpu.make_async_copy(add_ref, add_held, small_sems.at[1])
        add_copy.start()
        add_copy.wait()
    panel_copy.wait()
    p_high, p_low = halves(-panel_held[...])
    p_both = jnp.concatenate([p_high, p_low], axis=0)
    dot = functools.partial(jnp.dot, preferred_element_type=jnp.float32)
    for part in range(count):
        for two in range(2):
            copies[4 * part + 2 * two].wait()
            copies[4 * part + 2 * two + 1].wait()
            s_high, s_low = halves(slots[part, :, pl.ds(256 * two, 256)])
            wide = dot(p_both, s_high)
            got = wide[64:] + dot(p_high, s_low) + wide[:64]
            for step in range(2 * two, 2 * two + 2):
                block = got[:, 128 * (step % 2) : 128 * (step % 2 + 1)]
                if add_ref is not None and flips[part] == (0, 0):
                    block = block + jnp.where(q == step, add_held[...], 0.0)
                out_ref[part, step] = block


def product(flips, panel, solved, add=None):
    args = (panel, solved) + (() if add is None else (add,))
    count = len(flips)
    return pl.pallas_call(
        functools.partial(product_kernel, flips),
        out_shape=jax.ShapeDtypeStruct((count, 4, 64, 128), jnp.float32),
        in_specs=[pl.BlockSpec(memory_space=pl.ANY)] * len(args),
        out_specs=pl.BlockSpec(memory_space=pltpu.VMEM),
        scratch_shapes=[
            pltpu.VMEM((64, 512), jnp.float32),
            pltpu.VMEM((64, 128), jnp.float32),
            pltpu.VMEM((count, 512, 512), jnp.float32),
            pltpu.SemaphoreType.DMA((count, 4)),
            pltpu.SemaphoreType.DMA((2,)),
        ],
        compiler_params=pltpu.CompilerParams(vmem_limit_bytes=52 << 20),
        cost_estimate=pl.CostEstimate(flops=count * 10**8, bytes_accessed=count << 20, transcendentals=0),
    )(*args)


def sum_kernel(got_ref, first_ref, second_ref):
    total = got_ref[0]
    for q in range(1, 4):
        total = total + got_ref[q]
    first_ref[...] = jnp.concatenate([total[0, 0], total[1, 0]], axis=0)
    second_ref[...] = jnp.concatenate([total[0, 1], total[1, 1]], axis=0)


def pass_kernel(keep_ref, moved_ref, out_ref):
    out_ref[...] = keep_ref[0] + moved_ref[0]


def spread_kernel(keep_ref, moved_ref, passed_ref, out_ref):
    total = keep_ref[1] + moved_ref[1] + passed_ref[...]
    out_ref[:, 0] = total
    out_ref[:, 1] = total


def times(factor, blocks_ref):
    x = blocks_ref[...].reshape(1024, 128)
    f_high, f_low = halves(factor)
    x_high, x_low = halves(x)
    dot = functools.partial(jnp.dot, preferred_element_type=jnp.float32)
    wide = dot(jnp.concatenate([f_high, f_low], axis=0), x_high)
    rows = factor.shape[0]
    return wide[rows:] + dot(f_high, x_low) + wide[:rows]


def rows_kernel(step, mine_ref, theirs_ref, x_ref, *rest):
    out_ref = rest[-1]
    zh = lax.axis_index("zh")
    got = times(jnp.concatenate([mine_ref[0], theirs_ref[step]], axis=0), x_ref)
    got = jnp.where(zh == 0, got, jnp.concatenate([got[32:], got[:32]], axis=0))
    out_ref[...] = rest[0][...] - got if len(rest) == 2 else got


def last_kernel(factor_ref, x_ref, first_ref, out_ref):
    zh = lax.axis_index("zh")
    out_ref[0] = jnp.where(zh == 0, first_ref[:32], first_ref[32:])
    out_ref[1] = times(factor_ref[1], x_ref)


def in_vmem(kernel, shape, *args):
    vmem = pl.BlockSpec(memory_space=pltpu.VMEM)
    return pl.pallas_call(
        kernel,
        out_shape=jax.ShapeDtypeStruct(shape, jnp.float32),
        in_specs=[vmem] * len(args),
        out_specs=vmem,
        compiler_params=pltpu.CompilerParams(vmem_limit_bytes=8 << 20),
        cost_estimate=pl.CostEstimate(flops=10**6, bytes_accessed=10**6, transcendentals=0),
    )(*args)


def pair_up(index, mine, theirs):
    first = index == 0
    return jnp.stack([jnp.where(first, mine, theirs), jnp.where(first, theirs, mine)])


def gather_plane(block):
    copies = jnp.broadcast_to(block[None], (16,) + block.shape)
    return lax.all_to_all(copies, ("y", "x"), 0, 0, tiled=True)


def on_device(right_side, diag_inverse, coupling, panel, solved):
    b, core = (lax.axis_index(a) for a in ("b", "core"))
    swap = [(0, 1), (1, 0)]

    rows = lambda x: lax.dynamic_slice_in_dim(x, 16 * core, 16, 0)
    quarter = jnp.where(b == 1, rows(diag_inverse[0]), rows(coupling))
    quarter = lax.ppermute(quarter, ("zh",) + LINE, [(z, 15 - z) for z in range(16)])

    panel = panel.reshape(64, 512)
    moved = lax.ppermute(product(((1, 1), (0, 1)), panel, solved), "core", swap)
    keep = product(((1, 0), (0, 0)), panel, solved, right_side.reshape(64, 128))
    passed = lax.ppermute(in_vmem(pass_kernel, (4, 64, 128), keep, moved), "b", swap)
    copies = in_vmem(spread_kernel, (4, 2, 64, 128), keep, moved, passed).reshape(8, 64, 128)
    half = pair_up(core, quarter, lax.ppermute(quarter, "core", swap))
    other = pair_up(b, half, lax.ppermute(half, "b", swap)).reshape(2, 32, 1024)
    got_all = lax.all_to_all(copies, ("q", "zh"), 0, 0, tiled=True)
    got_all, other = lax.optimization_barrier((got_all, other))
    vmem = pl.BlockSpec(memory_space=pltpu.VMEM)
    first_res, second_part = pl.pallas_call(
        sum_kernel,
        out_shape=(jax.ShapeDtypeStruct((64, 128), jnp.float32),) * 2,
        in_specs=[vmem],
        out_specs=(vmem, vmem),
        compiler_params=pltpu.CompilerParams(vmem_limit_bytes=8 << 20),
    )(got_all.reshape(4, 2, 2, 32, 128))
    first_rows, second_rows = (functools.partial(rows_kernel, step) for step in range(2))
    first_sol = in_vmem(first_rows, (64, 128), diag_inverse, other, gather_plane(first_res))
    second_res = in_vmem(
        second_rows, (64, 128), coupling[None], other, gather_plane(first_sol), second_part
    )
    return in_vmem(last_kernel, (2, 32, 128), diag_inverse, gather_plane(second_res), first_sol)


def solution(mesh):
    fine = Mesh(mesh.devices.reshape(4, 4, 2, 4, 2, 2), ROWS + COLS)
    return jax.shard_map(
        on_device,
        mesh=fine,
        in_specs=(
            P(None, ROWS, COLS),
            P(None, ROWS, None),
            P(ROWS, None),
            P(None, ROWS, COLS),
            P(COLS, None),
        ),
        out_specs=P(None, ROWS, COLS),
        check_vma=False,
    )
```
